32 devices in a mesh: seq: 8 (over z, y), tp: 2 (over x), dp: 2 (over core).
Axes of the slice: x: 2, y: 2, z: 4, core: 2. Of those that a mesh axis runs over, the one named last changes fastest.
Arguments:
- codes: int32 [2, 2048], P('dp', 'seq'), may hold values from 0 to 4095
- targets: int32 [2, 2048], P('dp', 'seq'), may hold values from 0 to 4095
- tok_weights: int32 [2, 2048], P('dp', 'seq'), may hold values from 1 to 4
- group_ids: int32 [2, 2048], P('dp'), may hold values from 0 to 19, as said below
- labels: int32 [2, 2], replicated, may hold values from 0 to 999
- tables_w: float32 [5106, 1024], P(None, ('seq', 'dp')), may hold values from -6 to 6
- tables_m: float32 [5106, 1024], P(None, ('seq', 'dp')), may hold values from -0.0014648438 to 0.0014648438, as said below
- tables_v: float32 [5106, 1024], P(None, ('seq', 'dp')), may hold values from 5.820766e-11 to 2.3841858e-07, as said below
- ada_w: float32 [1024, 8192], P(('seq', 'dp')), may hold values from -0.1875 to 0.1875
- ada_m: float32 [1024, 8192], P(('seq', 'dp')), may hold values from -0.00390625 to 0.00390625
- ada_v: float32 [1024, 8192], P(('seq', 'dp')), may hold values from 5.9604645e-08 to 2.3841858e-07
- attn_w: float32 [4, 1024, 1024], P(None, ('seq', 'dp'), 'tp'), may hold values from -0.75 to 0.75
- attn_m: float32 [4, 1024, 1024], P(None, ('seq', 'dp'), 'tp'), may hold values from -0.00390625 to 0.00390625
- attn_v: float32 [4, 1024, 1024], P(None, ('seq', 'dp'), 'tp'), may hold values from 5.9604645e-08 to 2.3841858e-07
- mlp_w: float32 [2, 1024, 4096], P(None, ('seq', 'dp'), 'tp'), may hold values from -0.1875 to 0.1875
- mlp_m: float32 [2, 1024, 4096], P(None, ('seq', 'dp'), 'tp'), may hold values from -0.00390625 to 0.00390625
- mlp_v: float32 [2, 1024, 4096], P(None, ('seq', 'dp'), 'tp'), may hold values from 5.9604645e-08 to 2.3841858e-07
- head_w: float32 [1024, 4096], P(('seq', 'dp'), 'tp'), may hold values from -0.1875 to 0.1875
- head_m: float32 [1024, 4096], P(('seq', 'dp'), 'tp'), may hold values from -0.00390625 to 0.00390625
- head_v: float32 [1024, 4096], P(('seq', 'dp'), 'tp'), may hold values from 5.9604645e-08 to 2.3841858e-07
- small_w: float32 [2, 1024], P(None, 'tp'), may hold values from -8 to 8
- small_m: float32 [2, 1024], P(None, 'tp'), may hold values from -0.00390625 to 0.00390625
- small_v: float32 [2, 1024], P(None, 'tp'), may hold values from 5.9604645e-08 to 2.3841858e-07
Outputs:
- loss: float32 [], replicated
- grad_norm: float32 [], replicated
- tables_m_new: float32 [5106, 1024], P(None, ('seq', 'dp'))
- tables_v_new: float32 [5106, 1024], P(None, ('seq', 'dp'))
- tables_w_new: float32 [5106, 1024], P(None, ('seq', 'dp'))
- ada_m_new: float32 [1024, 8192], P(('seq', 'dp'))
- ada_v_new: float32 [1024, 8192], P(('seq', 'dp'))
- ada_w_new: float32 [1024, 8192], P(('seq', 'dp'))
- attn_m_new: float32 [4, 1024, 1024], P(None, ('seq', 'dp'), 'tp')
- attn_v_new: float32 [4, 1024, 1024], P(None, ('seq', 'dp'), 'tp')
- attn_w_new: float32 [4, 1024, 1024], P(None, ('seq', 'dp'), 'tp')
- attn_bf: bfloat16 [4, 1024, 1024], P(None, ('seq', 'dp'), 'tp')
- mlp_m_new: float32 [2, 1024, 4096], P(None, ('seq', 'dp'), 'tp')
- mlp_v_new: float32 [2, 1024, 4096], P(None, ('seq', 'dp'), 'tp')
- mlp_w_new: float32 [2, 1024, 4096], P(None, ('seq', 'dp'), 'tp')
- mlp_bf: bfloat16 [2, 1024, 4096], P(None, ('seq', 'dp'), 'tp')
- head_m_new: float32 [1024, 4096], P(('seq', 'dp'), 'tp')
- head_v_new: float32 [1024, 4096], P(('seq', 'dp'), 'tp')
- head_w_new: float32 [1024, 4096], P(('seq', 'dp'), 'tp')
- head_bf: bfloat16 [1024, 4096], P(('seq', 'dp'), 'tp')
- small_m_new: float32 [2, 1024], P(None, 'tp')
- small_v_new: float32 [2, 1024], P(None, 'tp')
- small_w_new: float32 [2, 1024], P(None, 'tp')
The draws below stay inside these ranges and needn't reach their ends.
Inputs may be any that keep to these rules, and one draw needn't show every extreme that they name: `group_ids`: each row holds 2 items of 1024 tokens, numbered in a rotation drawn for each row; tokens are ordered by scale, then by position of the item in the row; each item's scales follow one of VAR's two token plans (680 or 2240 tokens) scaled to its length, every scale 0 nonempty. `tables_m`: first moments of the tables, smaller on the code rows. `tables_v`: positive second moments of the tables, smaller on the code rows.
All inputs are finite; a program needn't handle non-finite values.
Results may differ from the reference program's by a relative error of at most 0.0035.
The reference program's roundings to bfloat16 on the way count: a program that leaves them out, or rounds other values in their place, can miss the bound.
Values may be sent and summed in bfloat16 or wider, within the bound.
A program may use at most 320 MiB of HBM per device.

```python
import math
import jax
import jax.numpy as jnp
from jax import lax

D = 1024
HEADS = 16
HD = 64
FF = 4096
V = 4096
NCLS = 1000
LEVELS = 10
STEP = 3
ROW_TOK = 2048
ROWS = 2
ITEMS = 2
TROWS = 5106


def row_scale():
    rows = jnp.arange(TROWS)
    return jnp.where(rows < V, 1.0 / (128.0 * D), 1.0 / (4.0 * D)).astype(jnp.float32)


def draw_tables_m(key, part):
    key = jax.random.fold_in(key, 11)
    values = jnp.clip(jax.random.normal(key, (TROWS, D), jnp.float32), -6.0, 6.0)
    return values * row_scale()[:, None]


def draw_tables_v(key, part):
    key = jax.random.fold_in(key, 12)
    scale = row_scale()[:, None]
    spread = jnp.exp(jax.random.uniform(key, (TROWS, D), jnp.float32, 0.0, math.log(4.0)))
    return spread * scale * scale


def draw_group_ids(key, part):
    key = jax.random.fold_in(key, 13)
    length = ROW_TOK // ITEMS
    small_cum = jnp.array([1, 5, 14, 30, 55, 91, 155, 255, 424, 680], jnp.int32)
    large_cum = jnp.array([1, 5, 14, 30, 66, 147, 316, 640, 1216, 2240], jnp.int32)
    kinds = jax.random.randint(jax.random.fold_in(key, 1), (ROWS, ITEMS), 0, 2)
    turns = jax.random.randint(jax.random.fold_in(key, 2), (ROWS, 1), 0, ITEMS)
    cumul = jnp.where(kinds[..., None] == 0, small_cum[None, None, :], large_cum[None, None, :])
    whole = cumul[..., -1:]
    ends = (cumul * length + whole - 1) // whole
    starts = jnp.concatenate([jnp.zeros((ROWS, ITEMS, 1), jnp.int32), ends[..., :-1]], 2)
    counts = jnp.transpose(ends - starts, (0, 2, 1)).reshape(ROWS, LEVELS * ITEMS)
    offsets = jnp.cumsum(counts, 1)
    places = jnp.arange(ROW_TOK, dtype=jnp.int32)
    index = jnp.sum((offsets[:, None, :] <= places[None, :, None]).astype(jnp.int32), 2)
    item_num = (index % ITEMS + turns) % ITEMS
    return (item_num * LEVELS + index // ITEMS).astype(jnp.int32)


def set_ends(drawn, key, low, largest):
    longest = drawn.shape.index(max(drawn.shape))
    spots = []
    for shift in (0, 1):
        where = [jax.random.randint(jax.random.fold_in(key, axis), (), 0, length) for axis, length in enumerate(drawn.shape)]
        where[longest] = (where[longest] + shift) % drawn.shape[longest]
        spots.append(tuple(where))
    return drawn.at[spots[0]].set(low).at[spots[1]].set(largest)


def block_scale(stream_key, dims, cuts, low, largest):
    def one(dim, parts):
        draws = jax.random.uniform(jax.random.fold_in(jax.random.fold_in(stream_key, 6), dim), (parts,), jnp.float32, low / len(cuts), largest / len(cuts))
        return jnp.repeat(jnp.exp(draws), dims[dim] // parts).reshape((-1,) + (1,) * (len(dims) - dim - 1))

    loudness = one(*cuts[0])
    for cut in cuts[1:]:
        loudness = loudness * one(*cut)
    return loudness


def noise(own_key, extent, scale, most, shards=(), kind=jnp.bfloat16):
    gain = block_scale(own_key, extent, shards, -0.22, 0.18) if shards else 1.0
    values = jax.random.normal(own_key, extent, jnp.float32) * scale * gain
    return jnp.minimum(jnp.maximum(values, -most), most).astype(kind)


def setup_inputs(seed: int = 0) -> dict:
    arg_keys = jax.random.split(jax.random.key(seed), 24)
    codes = set_ends(jax.random.randint(arg_keys[0], (ROWS, ROW_TOK), 0, V), jax.random.fold_in(arg_keys[0], 1), 0, V - 1).astype(jnp.int32)
    targets = set_ends(jax.random.randint(arg_keys[1], (ROWS, ROW_TOK), 0, V), jax.random.fold_in(arg_keys[1], 1), 0, V - 1).astype(jnp.int32)
    tok_weights = set_ends(jax.random.randint(arg_keys[2], (ROWS, ROW_TOK), 1, 5), jax.random.fold_in(arg_keys[2], 1), 1, 4).astype(jnp.int32)
    group_ids = draw_group_ids(jax.random.fold_in(arg_keys[23], 71), 0)
    labels = set_ends(jax.random.randint(arg_keys[4], (ROWS, ITEMS), 0, NCLS), jax.random.fold_in(arg_keys[4], 1), 0, NCLS - 1).astype(jnp.int32)
    tables_w = noise(arg_keys[5], (TROWS, D), 1.0, 6.0, ((1, 16),), jnp.float32)
    tables_m = draw_tables_m(jax.random.fold_in(arg_keys[23], 71), 0)
    tables_v = draw_tables_v(jax.random.fold_in(arg_keys[23], 71), 0)
    ada_w = noise(arg_keys[8], (D, 8 * D), D ** -0.5, 0.1875, ((0, 16),), jnp.float32)
    ada_m = noise(arg_keys[9], (D, 8 * D), (1 / (4 * D)), 0.00390625, ((0, 16),), jnp.float32)
    ada_v = jnp.clip(jnp.exp(math.log(2.384185791015625e-07) - 1.3862944 * jax.random.uniform(arg_keys[10], (D, 8 * D), jnp.float32) ** block_scale(arg_keys[10], (D, 8 * D), ((0, 16),), -0.2, 0.2)), 5.960464477539063e-08, 2.384185791015625e-07)
    attn_w = noise(arg_keys[11], (4, D, D), (D // 16) ** -0.5, 0.75, ((1, 16), (2, 2)), jnp.float32)
    attn_m = noise(arg_keys[12], (4, D, D), (1 / (4 * D)), 0.00390625, ((1, 16), (2, 2)), jnp.float32)
    attn_v = jnp.clip(jnp.exp(math.log(2.384185791015625e-07) - 1.3862944 * jax.random.uniform(arg_keys[13], (4, D, D), jnp.float32) ** block_scale(arg_keys[13], (4, D, D), ((1, 16), (2, 2)), -0.2, 0.2)), 5.960464477539063e-08, 2.384185791015625e-07)
    mlp_w = noise(arg_keys[14], (2, D, FF), D ** -0.5, 0.1875, ((1, 16), (2, 2)), jnp.float32)
    mlp_m = noise(arg_keys[15], (2, D, FF), (1 / (4 * D)), 0.00390625, ((1, 16), (2, 2)), jnp.float32)
    mlp_v = jnp.clip(jnp.exp(math.log(2.384185791015625e-07) - 1.3862944 * jax.random.uniform(arg_keys[16], (2, D, FF), jnp.float32) ** block_scale(arg_keys[16], (2, D, FF), ((1, 16), (2, 2)), -0.2, 0.2)), 5.960464477539063e-08, 2.384185791015625e-07)
    head_w = noise(arg_keys[17], (D, V), D ** -0.5, 0.1875, ((0, 16), (1, 2)), jnp.float32)
    head_m = noise(arg_keys[18], (D, V), (1 / (4 * D)), 0.00390625, ((0, 16), (1, 2)), jnp.float32)
    head_v = jnp.clip(jnp.exp(math.log(2.384185791015625e-07) - 1.3862944 * jax.random.uniform(arg_keys[19], (D, V), jnp.float32) ** block_scale(arg_keys[19], (D, V), ((0, 16), (1, 2)), -0.2, 0.2)), 5.960464477539063e-08, 2.384185791015625e-07)
    small_w = noise(arg_keys[20], (2, D), 2.0, 8.0, ((1, 2),), jnp.float32)
    small_m = noise(arg_keys[21], (2, D), (1 / (4 * D)), 0.00390625, ((1, 2),), jnp.float32)
    small_v = jnp.clip(jnp.exp(math.log(2.384185791015625e-07) - 1.3862944 * jax.random.uniform(arg_keys[22], (2, D), jnp.float32) ** block_scale(arg_keys[22], (2, D), ((1, 2),), -0.2, 0.2)), 5.960464477539063e-08, 2.384185791015625e-07)
    return {"codes": codes, "targets": targets, "tok_weights": tok_weights, "group_ids": group_ids, "labels": labels, "tables_w": tables_w, "tables_m": tables_m, "tables_v": tables_v, "ada_w": ada_w, "ada_m": ada_m, "ada_v": ada_v, "attn_w": attn_w, "attn_m": attn_m, "attn_v": attn_v, "mlp_w": mlp_w, "mlp_m": mlp_m, "mlp_v": mlp_v, "head_w": head_w, "head_m": head_m, "head_v": head_v, "small_w": small_w, "small_m": small_m, "small_v": small_v}


highest = lax.Precision.HIGHEST

@jax.custom_vjp
def low(v):
    return lax.optimization_barrier(v.astype(jnp.bfloat16)).astype(jnp.float32)

@jax.custom_vjp
def low_back(v):
    return v

def low_keep(v):
    return (low(v), None)

def low_pass(kept, grad):
    return (grad,)

def back_keep(v):
    return (v, None)

def back_low(kept, grad):
    return (low(grad),)
low.defvjp(low_keep, low_pass)
low_back.defvjp(back_keep, back_low)

def layer_norm(value):
    centered = value - lax.optimization_barrier(jnp.mean(value, -1, keepdims=True))
    return centered * lax.rsqrt(lax.optimization_barrier(jnp.mean(centered * centered, -1, keepdims=True)) + 1e-06)

def unit_rows(value):
    return value * lax.rsqrt(lax.optimization_barrier(jnp.mean(value * value, -1, keepdims=True)) + 1e-06)

def attend_row(queries, keys, values, groups):
    block_rows = min(256, ROW_TOK)
    count = ROW_TOK // block_rows

    def block(inputs):
        query_block, group_block = inputs
        scores = low_back(jnp.einsum('qhd,khd->hqk', query_block, keys, precision=highest))
        same = group_block[:, None] // LEVELS == groups[None, :] // LEVELS
        allowed = same & (groups[None, :] <= group_block[:, None])
        scores = jnp.where(allowed[None], scores, -1e+30)
        probs = jnp.exp(scores - jax.nn.logsumexp(scores, -1, keepdims=True))
        return jnp.einsum('hqk,khd->qhd', low(probs), values, precision=highest)
    outs = lax.map(jax.checkpoint(block), (queries.reshape(count, block_rows, HEADS, HD), groups.reshape(count, block_rows)))
    return outs.reshape(ROW_TOK, HEADS, HD)

def adamw(weight, first, second, grad, rate):
    first = 0.5 * first + 0.5 * grad
    second = 0.5 * second + 0.5 * grad * grad
    fix = 1.0 - 0.5 ** STEP
    update = first / fix / (jnp.sqrt(second / fix) + 1e-08)
    return (first, second, weight - rate * (update + 0.05 * weight))

def reference(codes, targets, tok_weights, group_ids, labels, tables_w, tables_m, tables_v, ada_w, ada_m, ada_v, attn_w, attn_m, attn_v, mlp_w, mlp_m, mlp_v, head_w, head_m, head_v, small_w, small_m, small_v):
    level = group_ids % LEVELS
    item = group_ids // LEVELS

    def forward(tables, ada, attn, mlp, head, small):
        table_low = low(tables)
        ada_low = low(ada)
        attn_low = low(attn)
        mlp_low = low(mlp)
        head_low = low(head)
        resid = table_low[codes] + table_low[V + NCLS + level]
        cond = table_low[V + labels]
        silu_cond = low(jax.nn.silu(cond))
        mods = jnp.einsum('rid,de->rie', silu_cond, ada_low, precision=highest)
        tok_mods = jax.vmap(lambda table, index: table[index])(mods, item)
        shift1, scale1, gate1, shift2, scale2, gate2, shift3, scale3 = jnp.split(tok_mods, 8, axis=-1)
        h_one = low(layer_norm(resid) * (1.0 + scale1) + shift1)
        q_raw = low_back(jnp.einsum('rnd,dc->rnc', h_one, attn_low[0], precision=highest) + small[0])
        k_raw = low_back(jnp.einsum('rnd,dc->rnc', h_one, attn_low[1], precision=highest))
        v_raw = low_back(jnp.einsum('rnd,dc->rnc', h_one, attn_low[2], precision=highest) + small[1])
        shape = (ROWS, ROW_TOK, HEADS, HD)
        q_heads = low(unit_rows(q_raw.reshape(shape)) * 0.25)
        k_heads = low(unit_rows(k_raw.reshape(shape)))
        v_heads = low(v_raw.reshape(shape))
        outs = jnp.stack([attend_row(q_heads[row], k_heads[row], v_heads[row], group_ids[row]) for row in range(ROWS)])
        heads_out = low(low_back(outs.reshape(ROWS, ROW_TOK, D)))
        attn_out = low_back(jnp.einsum('rnc,dc->rnd', heads_out, attn_low[3], precision=highest))
        x_one = resid + gate1 * attn_out
        h_two = low(layer_norm(x_one) * (1.0 + scale2) + shift2)
        up_val = low_back(jnp.einsum('rnd,df->rnf', h_two, mlp_low[0], precision=highest))
        act = low(jax.nn.gelu(up_val, approximate=True))
        mlp_out = low_back(jnp.einsum('rnf,df->rnd', act, mlp_low[1], precision=highest))
        x_two = x_one + gate2 * mlp_out
        h_three = low(layer_norm(x_two) * (1.0 + scale3) + shift3)
        logits = low_back(jnp.einsum('rnd,dv->rnv', h_three, head_low, precision=highest))
        log_total = jax.nn.logsumexp(logits, -1)
        target_logit = jnp.take_along_axis(logits, targets[..., None], -1)[..., 0]
        token_loss = log_total - 0.9 * target_logit - 0.1 * lax.optimization_barrier(jnp.mean(logits, -1))
        weights = tok_weights.astype(jnp.float32)
        return 128.0 * jnp.sum(weights * token_loss) / jnp.sum(weights)
    params = (tables_w, ada_w, attn_w, mlp_w, head_w, small_w)
    loss, pullback = jax.vjp(forward, *params)
    grads = pullback(jnp.ones((), jnp.float32))
    grad_norm = jnp.sqrt(sum((jnp.sum(grad * grad) for grad in grads)))
    factor = jnp.minimum(1.0, 1.0 / (grad_norm + 1e-06))
    firsts = (tables_m, ada_m, attn_m, mlp_m, head_m, small_m)
    seconds = (tables_v, ada_v, attn_v, mlp_v, head_v, small_v)
    rates = (0.3, 0.03, 0.1, 0.02, 0.03, 0.5)
    news = [adamw(params[index], firsts[index], seconds[index], grads[index] * factor, rates[index]) for index in range(6)]
    tables_n, ada_n, attn_n, mlp_n, head_n, small_n = news
    return (loss, grad_norm, tables_n[0], tables_n[1], tables_n[2], ada_n[0], ada_n[1], ada_n[2], attn_n[0], attn_n[1], attn_n[2], attn_n[2].astype(jnp.bfloat16), mlp_n[0], mlp_n[1], mlp_n[2], mlp_n[2].astype(jnp.bfloat16), head_n[0], head_n[1], head_n[2], head_n[2].astype(jnp.bfloat16), small_n[0], small_n[1], small_n[2])
```

```python
import functools
import math

import jax
import jax.numpy as jnp
from jax import lax
from jax.experimental import pallas as pl
from jax.experimental.pallas import tpu as pltpu
from jax.sharding import PartitionSpec as P

HD = 64
V = 4096
NCLS = 1000
LEVELS = 10
STEP = 3
AXES = ("seq", "tp", "dp")
BLOCKED = -30000.0


def place(axes, sizes, index):
    coords = {axis: lax.axis_index(axis) for axis in AXES}
    for axis in reversed(axes):
        coords[axis] = lax.rem(index, sizes[axis])
        index = index // sizes[axis]
    return tuple(coords[axis] for axis in AXES)


def linear(axes, sizes):
    index = 0
    for axis in axes:
        index = index * sizes[axis] + lax.axis_index(axis)
    return index


def direct_kernel(axes, sizes, spreads, *refs):
    count = math.prod(sizes[axis] for axis in axes)
    number = len(spreads)
    sources, targets = refs[:number], refs[number : 2 * number]
    send, recv, own = refs[2 * number :]
    me = linear(axes, sizes)
    barrier = pltpu.get_barrier_semaphore()

    def peer_at(step):
        return lax.rem(me + step, count)

    def greet(step, carry):
        pl.semaphore_signal(
            barrier,
            inc=1,
            device_id=place(axes, sizes, peer_at(step)),
            device_id_type=pl.DeviceIdType.MESH,
        )
        return carry

    lax.fori_loop(1, count, greet, 0)
    pl.semaphore_wait(barrier, count - 1)

    def ends(index, peer):
        source = sources[index].at[peer] if spreads[index] else sources[index]
        return source, targets[index].at[me]

    def copy_at(step, index):
        peer = peer_at(step)
        source, target = ends(index, peer)
        return pltpu.make_async_remote_copy(
            src_ref=source,
            dst_ref=target,
            send_sem=send.at[index, step],
            recv_sem=recv.at[index, step],
            device_id=place(axes, sizes, peer),
            device_id_type=pl.DeviceIdType.MESH,
        )

    def start(step, carry):
        for index in range(number):
            copy_at(step, index).start()
        return carry

    def finish(step, carry):
        for index in range(number):
            copy_at(step, index).wait()
        return carry

    lax.fori_loop(1, count, start, 0)
    local = []
    for index in range(number):
        source, target = ends(index, me)
        local.append(pltpu.make_async_copy(source, target, own.at[index]))
        local[-1].start()
    lax.fori_loop(1, count, finish, 0)
    for copy in local:
        copy.wait()


def direct(payloads, axes, sizes, number):
    count = math.prod(sizes[axis] for axis in axes)
    values = [value for value, _ in payloads]
    spreads = tuple(spread for _, spread in payloads)
    shapes = [
        jax.ShapeDtypeStruct(value.shape if spread else (count,) + value.shape, value.dtype)
        for value, spread in payloads
    ]
    return pl.pallas_call(
        functools.partial(direct_kernel, axes, sizes, spreads),
        out_shape=shapes,
        in_specs=[pl.BlockSpec(memory_space=pl.ANY)] * len(values),
        out_specs=[pl.BlockSpec(memory_space=pl.ANY)] * len(values),
        scratch_shapes=[
            pltpu.SemaphoreType.DMA((len(values), count)),
            pltpu.SemaphoreType.DMA((len(values), count)),
            pltpu.SemaphoreType.DMA((len(values),)),
        ],
        compiler_params=pltpu.CompilerParams(collective_id=number, has_side_effects=True),
        name=f"direct_{number}",
    )(*values)


def pairs_kernel(sizes, heads, tokens, outward, count, *refs):
    sources, targets = refs[:count], refs[count : 2 * count]
    send, recv, own = refs[2 * count :]
    pairs = 2 * heads
    half = tokens // 2
    at_seq, at_tp, at_dp = (lax.axis_index(axis) for axis in AXES)
    base = at_seq // pairs * pairs
    me = lax.rem(at_seq, pairs)

    def device(peer):
        return (base + peer, at_tp, at_dp)

    barrier = pltpu.get_barrier_semaphore()
    for step in range(1, pairs):
        pl.semaphore_signal(
            barrier,
            inc=1,
            device_id=device(lax.rem(me + step, pairs)),
            device_id_type=pl.DeviceIdType.MESH,
        )
    pl.semaphore_wait(barrier, pairs - 1)

    def ends(index, piece, pair, chunk):
        row = lax.rem(pair // heads + at_dp, 2)
        inner = pl.ds(pl.multiple_of((row * 2 + piece) * half, half), half)
        outer = pl.ds(
            pl.multiple_of(chunk * tokens + lax.rem(piece + at_tp, 2) * half, half), half
        )
        head = lax.rem(pair, heads)
        if outward:
            return sources[index].at[:, head, :, inner], targets[index].at[:, :, outer]
        return sources[index].at[:, :, outer], targets[index].at[:, head, :, inner]

    copies = []
    for step in range(1, pairs):
        peer = lax.rem(me + step, pairs)
        pair, chunk = (peer, me) if outward else (me, peer)
        for index in range(count):
            for piece in range(2):
                source, target = ends(index, piece, pair, chunk)
                copies.append(
                    pltpu.make_async_remote_copy(
                        src_ref=source,
                        dst_ref=target,
                        send_sem=send.at[index, piece, step],
                        recv_sem=recv.at[index, piece, step],
                        device_id=device(peer),
                        device_id_type=pl.DeviceIdType.MESH,
                    )
                )
                copies[-1].start()
    for index in range(count):
        for piece in range(2):
            source, target = ends(index, piece, me, me)
            copies.append(pltpu.make_async_copy(source, target, own.at[index, piece]))
            copies[-1].start()
    for copy in copies:
        copy.wait()


def pair_exchange(values, sizes, heads, tokens, outward, number):
    pairs = 2 * heads
    if outward:
        shapes = [(v.shape[0], v.shape[2], pairs * tokens) for v in values]
    else:
        shapes = [(v.shape[0], heads, v.shape[1], 2 * tokens) for v in values]
    count = len(values)
    return pl.pallas_call(
        functools.partial(pairs_kernel, sizes, heads, tokens, outward, count),
        out_shape=[jax.ShapeDtypeStruct(s, v.dtype) for s, v in zip(shapes, values)],
        in_specs=[pl.BlockSpec(memory_space=pl.ANY)] * count,
        out_specs=[pl.BlockSpec(memory_space=pl.ANY)] * count,
        scratch_shapes=[
            pltpu.SemaphoreType.DMA((count, 2, pairs)),
            pltpu.SemaphoreType.DMA((count, 2, pairs)),
            pltpu.SemaphoreType.DMA((count, 2)),
        ],
        compiler_params=pltpu.CompilerParams(collective_id=number, has_side_effects=True),
        name=f"pairs_{number}",
    )(*values)


def swapped(value, axis):
    return lax.ppermute(value, axis, [(0, 1), (1, 0)])


def group_gather(value):
    row = jnp.concatenate([value, swapped(value, "tp")], 0)
    return jnp.concatenate([row, swapped(row, "dp")], 0)


def remote(source, target, send, recv, device):
    return pltpu.make_async_remote_copy(
        src_ref=source,
        dst_ref=target,
        send_sem=send,
        recv_sem=recv,
        device_id=device,
        device_id_type=pl.DeviceIdType.MESH,
    )


def reduce_steps(x, out, scratch, sizes):
    from_y, staged, from_low, from_high, b_staged, b_low, b_high, b_y, total, send, recv = scratch
    deep = sizes["seq"] // 2
    at_seq, at_tp, at_dp = (lax.axis_index(axis) for axis in AXES)
    z, y = at_seq // 2, lax.rem(at_seq, 2)
    beside = (at_seq + 1 - 2 * y, at_tp, at_dp)
    above = (lax.min(at_seq + 2, sizes["seq"] - 1), at_tp, at_dp)
    below = (lax.max(at_seq - 2, 0), at_tp, at_dp)
    split = from_y.shape[2]
    first, second = pl.ds(0, split), pl.ds(split, x.shape[3] - split)

    def block(index):
        return lax.rem(z + index, deep)

    def copy(kind, slot, source, target, device):
        return remote(source, target, send.at[kind, slot], recv.at[kind, slot], device)

    def y_copy(index):
        return copy(0, index, x.at[block(index), 1 - y, :, first], from_y.at[index], beside)

    def up_copy(turn):
        return copy(1, turn - 1, staged.at[deep - turn], from_low.at[turn - 1], above)

    def down_copy(turn):
        return copy(2, turn - 1, staged.at[turn], from_high.at[turn - 1], below)

    def b_up_copy(turn):
        return copy(3, turn - 1, b_staged.at[deep - turn], b_low.at[turn - 1], above)

    def b_down_copy(turn):
        return copy(4, turn - 1, b_staged.at[turn], b_high.at[turn - 1], below)

    def b_y_copy():
        return copy(5, 0, b_staged.at[0, 1 - y], b_y, beside)

    def goes_up(turn):
        return (z <= turn - 1) & (z < deep - 1)

    def goes_down(turn):
        return (z >= deep - turn) & (z > 0)

    def move(turn, went, index, there, arrived, received, started, b):
        @pl.when(went)
        def _():
            if b:
                b_staged[index] = x[block(index), :, :, second]
            else:
                y_copy(index).wait_recv()
                staged[index] = x[block(index), y, :, first] + from_y[index]
            if turn > 1:

                @pl.when(there)
                def _():
                    arrived(turn - 1).wait_recv()
                    if b:
                        b_staged[index] += received[turn - 2]
                    else:
                        staged[index] += received[turn - 2]

            started(turn).start()

    def main(turn):
        move(turn, goes_up(turn), deep - turn, z > 0, up_copy, from_low, up_copy, False)
        move(turn, goes_down(turn), turn, z < deep - 1, down_copy, from_high, down_copy, False)

    def rest(turn):
        move(turn, goes_up(turn), deep - turn, z > 0, b_up_copy, b_low, b_up_copy, True)
        move(turn, goes_down(turn), turn, z < deep - 1, b_down_copy, b_high, b_down_copy, True)

    def begin():
        for turn in range(deep - 1):
            y_copy(lax.select(z < deep // 2, deep - 1 - turn, turn + 1)).start()
        y_copy(0).start()
        rest(1)

    def rest_end():
        b_staged[0] = x[z, :, :, second]

        @pl.when(z > 0)
        def _():
            b_up_copy(deep - 1).wait_recv()
            b_staged[0] += b_low[deep - 2]

        @pl.when(z < deep - 1)
        def _():
            b_down_copy(deep - 1).wait_recv()
            b_staged[0] += b_high[deep - 2]

        b_y_copy().start()

    def middle(turn):
        main(turn)
        if turn < deep - 1:
            rest(turn + 1)
        else:
            rest_end()

    columns = x.shape[3]
    half = total.shape[0] // 2
    place_in = pl.ds(pl.multiple_of(at_dp * columns, 128), columns)

    def core_copy():
        given = total.at[pl.ds(pl.multiple_of((1 - at_dp) * half, half), half)]
        return copy(5, 1, given, out.at[:, place_in], (at_seq, at_tp, 1 - at_dp))

    def main_end():
        y_copy(0).wait_recv()
        total[:, first] = x[z, y, :, first] + from_y[0]

        @pl.when(z > 0)
        def _():
            up_copy(deep - 1).wait_recv()
            total[:, first] += from_low[deep - 2]

        @pl.when(z < deep - 1)
        def _():
            down_copy(deep - 1).wait_recv()
            total[:, first] += from_high[deep - 2]

    def finish():
        b_y_copy().wait_recv()
        total[:, second] = b_staged[0, y] + b_y[...]
        core_copy().start()
        out[:, place_in] = total[pl.ds(pl.multiple_of(at_dp * half, half), half), :]
        core_copy().wait()
        for index in range(deep):
            y_copy(index).wait_send()
        b_y_copy().wait_send()
        for turn in range(1, deep):

            @pl.when(goes_up(turn))
            def _():
                up_copy(turn).wait_send()
                b_up_copy(turn).wait_send()

            @pl.when(goes_down(turn))
            def _():
                down_copy(turn).wait_send()
                b_down_copy(turn).wait_send()

    turns = [functools.partial(middle, turn) for turn in range(1, deep)]
    return [begin] + turns + [main_end, finish]


def reduce_scratch(value):
    deep, _, rows, columns = value.shape
    split = max(128, columns * 3 // 4 // 128 * 128)
    rest = columns - split
    kind = value.dtype
    return [
        pltpu.VMEM((deep, rows, split), kind),
        pltpu.VMEM((deep, rows, split), kind),
        pltpu.VMEM((deep - 1, rows, split), kind),
        pltpu.VMEM((deep - 1, rows, split), kind),
        pltpu.VMEM((deep, 2, rows, rest), kind),
        pltpu.VMEM((deep - 1, 2, rows, rest), kind),
        pltpu.VMEM((deep - 1, 2, rows, rest), kind),
        pltpu.VMEM((rows, rest), kind),
        pltpu.VMEM((rows, columns), kind),
        pltpu.SemaphoreType.DMA((6, deep)),
        pltpu.SemaphoreType.DMA((6, deep)),
    ]


def reduced(value):
    rows, columns = value.shape[2:]
    return jax.ShapeDtypeStruct((rows // 2, 2 * columns), value.dtype)


def room(*shapes):
    size = 0
    for shape, kind in shapes:
        padded = list(shape)
        padded[-1] = -(-padded[-1] // 128) * 128
        if len(padded) > 1:
            padded[-2] = -(-padded[-2] // 16) * 16
        size += math.prod(padded) * jnp.dtype(kind).itemsize
    return min(size + 6 * 1024 * 1024, 60 * 1024 * 1024)


def sizes_of(scratch):
    return [(item.shape, item.dtype) for item in scratch if item.memory_space == pltpu.VMEM]


PIECES = 4


def normed_of(x):
    centered = x - jnp.mean(x, -1, keepdims=True)
    factor = lax.rsqrt(jnp.mean(centered * centered, -1, keepdims=True) + 1e-06)
    return centered * factor, factor


def stage_kernel(mode, parts, items, sizes, given, jobs, *refs):
    refs = list(refs)

    def take(count):
        taken, refs[:count] = refs[:count], []
        return taken

    terms, *values = take(given)
    mods, select = take(2)
    sums_in = take(jobs)
    gathers = mode != "last"
    first_out, second_out = take(2)
    gathered = take(1)[0] if gathers else None
    sums_out = take(jobs)
    from_core, passed, from_x, send, recv = take(5)
    scratch = [take(11) for _ in range(jobs)]
    block = terms.shape[1]
    size = block // PIECES
    at_seq, at_tp, at_dp = (lax.axis_index(axis) for axis in AXES)
    core, across = (at_seq, at_tp, 1 - at_dp), (at_seq, 1 - at_tp, at_dp)

    barrier = pltpu.get_barrier_semaphore()

    def greet(device):
        pl.semaphore_signal(barrier, inc=1, device_id=device, device_id_type=pl.DeviceIdType.MESH)

    greet(core)
    greet(across)
    expected = 2
    if jobs:
        z, y, deep = at_seq // 2, lax.rem(at_seq, 2), sizes["seq"] // 2
        greet((at_seq + 1 - 2 * y, at_tp, at_dp))

        @pl.when(z > 0)
        def _():
            greet((at_seq - 2, at_tp, at_dp))

        @pl.when(z < deep - 1)
        def _():
            greet((at_seq + 2, at_tp, at_dp))

        expected = 3 + lax.min(z, 1) + lax.min(deep - 1 - z, 1)
    pl.semaphore_wait(barrier, expected)

    def rows(piece):
        return pl.ds(piece * size, size)

    def copy(kind, piece, source, target, device):
        return remote(source, target, send.at[kind, piece], recv.at[kind, piece], device)

    def core_copy(piece):
        return copy(0, piece, terms.at[pl.ds(2, 2), rows(piece)], from_core.at[:, rows(piece)], core)

    def x_copy(piece):
        return copy(1, piece, passed.at[rows(piece)], from_x.at[rows(piece)], across)

    def share_x(piece):
        return copy(2, piece, gathered.at[0, rows(piece)], gathered.at[1, rows(piece)], across)

    def share_core(piece):
        return copy(3, piece, gathered.at[0, rows(piece)], gathered.at[2, rows(piece)], core)

    def forward_core(piece):
        return copy(4, piece, gathered.at[1, rows(piece)], gathered.at[3, rows(piece)], core)

    waiting = []
    for index in range(jobs):
        waiting.append(reduce_steps(sums_in[index], sums_out[index], scratch[index], sizes))

    def advance():
        for steps in waiting:
            if steps:
                steps.pop(0)()

    for piece in range(PIECES):
        core_copy(piece).start()
    advance()
    for piece in range(PIECES):
        at = rows(piece)
        core_copy(piece).wait_recv()
        passed[at, :] = terms[1, at, :] + from_core[1, at, :]
        x_copy(piece).start()
    for piece in range(PIECES):
        at = rows(piece)
        chosen = [select[at, i : i + 1] for i in range(items)]

        def mod(part):
            return sum(chosen[i] * mods[i * 8 + part : i * 8 + part + 1, :] for i in range(items))

        def tally(index, value):
            for i in range(items):
                slot = pl.ds(index * items + i, 1)
                part = jnp.sum(chosen[i] * value, 0, keepdims=True)
                if piece == 0:
                    second_out[slot, :] = part
                else:
                    second_out[slot, :] += part

        x_copy(piece).wait_recv()
        total = terms[0, at, :] + from_core[0, at, :] + from_x[at, :]
        if mode == "forward":
            gate, shift, scale = parts
            x = values[0][at, :] + mod(gate) * total
            first_out[at, :] = total
            second_out[at, :] = x
            result = normed_of(x)[0] * (1.0 + mod(scale)) + mod(shift)
        else:
            normed, factor = normed_of(values[0][at, :])
            grad = total * (1.0 + mod(parts[0]))
            d_x = factor * (
                grad
                - jnp.mean(grad, -1, keepdims=True)
                - normed * jnp.mean(grad * normed, -1, keepdims=True)
            )
            if given > (3 if gathers else 2):
                d_x = d_x + values[-1][at, :]
            first_out[at, :] = d_x
            tally(0, total)
            tally(1, total * normed)
            if gathers:
                tally(2, d_x * values[1][at, :])
                result = d_x * mod(parts[1])
        if gathers:
            gathered[0, at, :] = result.astype(jnp.bfloat16)
            share_x(piece).start()
            share_core(piece).start()
        advance()
    if gathers:
        for piece in range(PIECES):
            share_x(piece).wait_recv()
            forward_core(piece).start()
    while any(waiting):
        advance()
    for piece in range(PIECES):
        core_copy(piece).wait_send()
        x_copy(piece).wait_send()
        if gathers:
            share_core(piece).wait_recv()
            forward_core(piece).wait_recv()
            share_x(piece).wait_send()
            share_core(piece).wait_send()
            forward_core(piece).wait_send()


def stage(mode, parts, items, sizes, terms, values, mods, select, sums, number):
    block, width = terms.shape[0] // 4, terms.shape[1]
    f32, gathers = jnp.float32, mode != "last"
    inputs = [terms.reshape(4, block, width), *values, mods, select, *sums]
    second = {"forward": block, "backward": 3 * items, "last": 2 * items}[mode]
    shapes = [
        jax.ShapeDtypeStruct((block, width), f32),
        jax.ShapeDtypeStruct((second, width), f32),
    ]
    if gathers:
        shapes.append(jax.ShapeDtypeStruct((4, block, width), jnp.bfloat16))
    shapes += [reduced(value) for value in sums]
    scratch = [
        pltpu.VMEM((2, block, width), f32),
        pltpu.VMEM((block, width), f32),
        pltpu.VMEM((block, width), f32),
        pltpu.SemaphoreType.DMA((5, PIECES)),
        pltpu.SemaphoreType.DMA((5, PIECES)),
    ]
    for value in sums:
        scratch += reduce_scratch(value)
    results = pl.pallas_call(
        functools.partial(
            stage_kernel, mode, parts, items, sizes, 1 + len(values), len(sums)
        ),
        out_shape=shapes,
        in_specs=[pl.BlockSpec(memory_space=pltpu.VMEM)] * len(inputs),
        out_specs=[pl.BlockSpec(memory_space=pltpu.VMEM)] * len(shapes),
        scratch_shapes=scratch,
        compiler_params=pltpu.CompilerParams(
            collective_id=number,
            has_side_effects=True,
            vmem_limit_bytes=room(
                *((value.shape, value.dtype) for value in inputs + shapes), *sizes_of(scratch)
            ),
        ),
        name=f"stage_{number}",
    )(*inputs)
    outs = list(results)
    if gathers:
        outs[2] = outs[2].reshape(4 * block, width)
    return outs


def outer_kernel(dims, *refs):
    out = refs[-1]
    start = 0
    for index, dim in enumerate(dims):
        left, right = refs[2 * index], refs[2 * index + 1]
        count = right.shape[1 - dim] // 256

        def tile(step, carry, left=left, right=right, dim=dim, start=start):
            at = pl.ds(pl.multiple_of(step * 256, 256), 256)
            part = right[at, :] if dim else right[:, at]
            product = lax.dot_general(
                left[...], part, (((0,), (dim,)), ((), ())), preferred_element_type=jnp.float32
            )
            out[:, pl.ds(pl.multiple_of(start + step * 256, 256), 256)] = product.astype(out.dtype)
            return carry

        lax.fori_loop(0, count, tile, 0)
        start += count * 256


def outer(pairs, kind):
    dims = tuple(dim for _, _, dim in pairs)
    columns = sum(right.shape[1 - dim] for _, right, dim in pairs)
    inputs = [value for left, right, _ in pairs for value in (left, right)]
    rows, depth = pairs[0][0].shape[1], pairs[0][0].shape[0]
    return pl.pallas_call(
        functools.partial(outer_kernel, dims),
        out_shape=jax.ShapeDtypeStruct((rows, columns), kind),
        in_specs=[pl.BlockSpec(memory_space=pltpu.VMEM)] * len(inputs),
        out_specs=pl.BlockSpec(memory_space=pltpu.VMEM),
        cost_estimate=pl.CostEstimate(
            flops=2 * rows * columns * depth, bytes_accessed=8 * rows * columns, transcendentals=0
        ),
        compiler_params=pltpu.CompilerParams(
            vmem_limit_bytes=room(
                *((value.shape, value.dtype) for value in inputs), ((rows, columns), kind)
            )
        ),
        name="outer",
    )(*inputs)


def tail_kernel(items, sizes, *refs):
    cols, mods, x, own_codes, own_levels, other_codes, other_levels = refs[:7]
    mods_out, mods_in, sum_out, codes_out, levels_out = refs[7:12]
    own_cols, other_cols, parts, mods_own, mods_other, mods_sum = refs[12:18]
    send, recv, near, across_send, across_recv = refs[18:23]
    scratch = refs[23:]
    axes = ("seq", "dp")
    seq = sizes["seq"]
    count = seq * 2
    me = linear(axes, sizes)
    at_seq, at_tp, at_dp = (lax.axis_index(axis) for axis in AXES)
    across = (at_seq, 1 - at_tp, at_dp)
    barrier = pltpu.get_barrier_semaphore()

    def greet_device(device):
        pl.semaphore_signal(barrier, inc=1, device_id=device, device_id_type=pl.DeviceIdType.MESH)

    def greet(step, carry):
        greet_device(place(axes, sizes, lax.rem(me + step, count)))
        return carry

    lax.fori_loop(1, count, greet, 0)
    greet_device(across)
    pl.semaphore_wait(barrier, count)

    def ends(index, peer):
        if index == 0:
            return mods.at[peer], mods_in.at[me]
        if index == 1:
            return cols.at[peer], own_cols.at[me]
        return mods_sum, mods_out.at[me]

    def copy_at(index, step):
        peer = lax.rem(me + step, count)
        return remote(
            *ends(index, peer), send.at[index, step], recv.at[index, step], place(axes, sizes, peer)
        )

    def over_peers(index, action):
        def one(step, carry):
            getattr(copy_at(index, step), action)()
            return carry

        lax.fori_loop(1, count, one, 0)

    steps = reduce_steps(x, sum_out, scratch, sizes)

    def advance():
        if steps:
            steps.pop(0)()

    owners, width, block = own_cols.shape
    tokens = owners * block
    chunk = 1024
    tile = 512

    def fill(columns, side, owner):
        value = columns[owner]
        at = pl.ds(pl.multiple_of(owner * block, block), block)
        for index in range(3):
            part = value.astype(jnp.bfloat16)
            parts[side, pl.ds(index * width, width), at] = part
            value = value - part.astype(jnp.float32)

    def products(side, ids, first, height):
        def one(step, total):
            at = pl.ds(pl.multiple_of(step * chunk, chunk), chunk)
            rows = lax.broadcasted_iota(jnp.int32, (height, chunk), 0) + first
            hot = jnp.where(rows == ids[:, at], 1.0, 0.0).astype(jnp.bfloat16)
            return total + lax.dot_general(
                parts[side, :, at], hot, (((1,), (1,)), ((), ())), preferred_element_type=jnp.float32
            )

        total = jnp.zeros((3 * width, height), jnp.float32)
        total = lax.fori_loop(0, tokens // chunk, one, total)
        return total[:width] + total[width : 2 * width] + total[2 * width :]

    def tiles(side, codes, base, number):
        def one(step, carry):
            first = pl.multiple_of((base + step) * tile, tile)
            at = pl.ds(first, tile)
            value = products(side, codes, first, tile)
            if side:
                codes_out[:, at] += value
            else:
                codes_out[:, at] = value
            return carry

        lax.fori_loop(0, number, one, 0)

    def passed_on(owner):
        return remote(
            own_cols.at[owner],
            other_cols.at[owner],
            across_send.at[owner],
            across_recv.at[owner],
            across,
        )

    local = [pltpu.make_async_copy(*ends(index, me), near.at[index]) for index in range(3)]
    for index in range(2):
        over_peers(index, "start")
        local[index].start()
    over_peers(0, "wait")
    local[0].wait()
    for row in range(2):
        mine = mods_in[row, :items]
        for position in range(1, seq):
            mine = mine + mods_in[position * 2 + row, :items]
        mods_own[row] = mine
    mods_exchange = remote(
        mods_own, mods_other, across_send.at[owners], across_recv.at[owners], across
    )
    mods_exchange.start()
    local[1].wait()
    passed_on(me).start()
    fill(own_cols, 0, me)
    mods_exchange.wait()
    mods_sum[...] = mods_own[...] + mods_other[...]
    over_peers(2, "start")
    local[2].start()
    advance()

    def arrived(step, carry):
        copy_at(1, step).wait()
        owner = lax.rem(me - step + count, count)
        passed_on(owner).start()
        fill(own_cols, 0, owner)
        return carry

    lax.fori_loop(1, count, arrived, 0)
    advance()
    half = V // tile // 2
    tiles(0, own_codes, 0, half)
    advance()

    def crossed(owner, carry):
        passed_on(owner).wait()
        fill(other_cols, 1, owner)
        return carry

    lax.fori_loop(0, count, crossed, 0)
    tiles(0, own_codes, half, half)
    levels_out[...] = products(0, own_levels, 0, levels_out.shape[1])
    levels_out[...] += products(1, other_levels, 0, levels_out.shape[1])
    advance()
    tiles(1, other_codes, 0, half)
    advance()
    tiles(1, other_codes, half, half)
    while steps:
        advance()
    over_peers(2, "wait")
    local[2].wait()


def tail_stage(cols, mods, items, x, ids, sizes, number):
    count, width, block = cols.shape
    f32 = jnp.float32
    inputs = [cols, mods, x, *ids]
    in_vmem = pl.BlockSpec(memory_space=pltpu.VMEM)
    pair = (2, items, mods.shape[2])
    shapes = [
        jax.ShapeDtypeStruct((count,) + pair, f32),
        jax.ShapeDtypeStruct(mods.shape, f32),
        reduced(x),
        jax.ShapeDtypeStruct((width, V), f32),
        jax.ShapeDtypeStruct((width, 128), f32),
    ]
    scratch = [
        pltpu.VMEM(cols.shape, f32),
        pltpu.VMEM(cols.shape, f32),
        pltpu.VMEM((2, 3 * width, count * block), jnp.bfloat16),
        pltpu.VMEM(pair, f32),
        pltpu.VMEM(pair, f32),
        pltpu.VMEM(pair, f32),
        pltpu.SemaphoreType.DMA((3, count)),
        pltpu.SemaphoreType.DMA((3, count)),
        pltpu.SemaphoreType.DMA((3,)),
        pltpu.SemaphoreType.DMA((count + 1,)),
        pltpu.SemaphoreType.DMA((count + 1,)),
    ] + reduce_scratch(x)
    return pl.pallas_call(
        functools.partial(tail_kernel, items, sizes),
        out_shape=shapes,
        in_specs=[in_vmem] * len(inputs),
        out_specs=[in_vmem] * len(shapes),
        scratch_shapes=scratch,
        compiler_params=pltpu.CompilerParams(
            collective_id=number,
            has_side_effects=True,
            vmem_limit_bytes=room(
                *((value.shape, value.dtype) for value in inputs + shapes), *sizes_of(scratch)
            ),
        ),
        name=f"tail_{number}",
    )(*inputs)


def chunks(total):
    return min(total, 512)


def forward_kernel(
    limit_ref, q_ref, k_ref, v_ref, qg_ref, kg_ref, o_ref, inv_ref, qa_ref, ka_ref, exps
):
    step = pl.program_id(0)
    width = o_ref.shape[1]
    keys = k_ref.shape[1]
    size = chunks(keys)

    @pl.when(step == 0)
    def _():
        extra = ka_ref.shape[0] - HD
        ka_ref[:HD, :] = k_ref[...]
        level = lax.broadcasted_iota(jnp.int32, (extra, keys), 0)
        ka_ref[HD:, :] = jnp.where(level == kg_ref[...], 1.0, 0.0).astype(jnp.bfloat16)
        qa_ref[:HD, :] = q_ref[...]
        level = lax.broadcasted_iota(jnp.int32, (extra, q_ref.shape[1]), 0)
        open_ = (level <= qg_ref[0:1, :]) & (level >= qg_ref[1:2, :])
        qa_ref[HD:, :] = jnp.where(open_, 0.0, BLOCKED).astype(jnp.bfloat16)

    query = qa_ref[:, pl.ds(pl.multiple_of(step * width, 128), width)]

    def first(chunk, total):
        at = pl.ds(pl.multiple_of(chunk * size, 128), size)
        scores = lax.dot_general(
            ka_ref[:, at], query, (((0,), (0,)), ((), ())), preferred_element_type=jnp.float32
        )
        expd = jnp.exp(scores)
        exps[at, :] = expd
        return total + jnp.sum(expd, 0, keepdims=True)

    limit = limit_ref[step]
    total = lax.fori_loop(0, limit, first, jnp.zeros((1, width), jnp.float32))
    inverse = 1.0 / total
    inv_ref[...] = inverse

    def second(chunk, out):
        at = pl.ds(pl.multiple_of(chunk * size, 128), size)
        probs = (exps[at, :] * inverse).astype(jnp.bfloat16)
        return out + jnp.dot(v_ref[:, at], probs, preferred_element_type=jnp.float32)

    out = lax.fori_loop(0, limit, second, jnp.zeros((HD, width), jnp.float32))
    o_ref[...] = out.astype(jnp.bfloat16)


def query_width(keys):
    return 256 if keys <= 4096 else 128


def whole(shape):
    return pl.BlockSpec(shape, lambda step: (0,) * len(shape))


def kind_block(value, kind):
    return pl.BlockSpec((None,) + value.shape[1:], lambda step: (kind, 0, 0))


def attend_forward(own, everyone, query_groups, key_groups, extra, limits):
    queries, keys = own.shape[2], everyone.shape[2]
    width = query_width(keys)
    depth = HD + extra

    def part(rows):
        return pl.BlockSpec((rows, width), lambda step: (0, step))

    return pl.pallas_call(
        forward_kernel,
        grid=(queries // width,),
        out_shape=(
            jax.ShapeDtypeStruct((HD, queries), jnp.bfloat16),
            jax.ShapeDtypeStruct((1, queries), jnp.float32),
            jax.ShapeDtypeStruct((depth, queries), jnp.bfloat16),
            jax.ShapeDtypeStruct((depth, keys), jnp.bfloat16),
        ),
        in_specs=[
            pl.BlockSpec(memory_space=pltpu.SMEM),
            kind_block(own, 0),
            kind_block(everyone, 1),
            kind_block(everyone, 2),
            whole(query_groups.shape),
            whole(key_groups.shape),
        ],
        out_specs=(part(HD), part(1), whole((depth, queries)), whole((depth, keys))),
        scratch_shapes=[pltpu.VMEM((keys, width), jnp.float32)],
        compiler_params=pltpu.CompilerParams(
            vmem_limit_bytes=room(
                *(((depth, count), jnp.bfloat16) for count in (queries, keys) * 4),
                ((keys, width), jnp.float32),
                ((4 * HD, keys), jnp.float32),
            )
        ),
        name="attend_forward",
    )(limits, own, everyone, everyone, query_groups, key_groups)


def backward_kernel(
    limit_ref, qa_ref, ka_ref, v_ref, do_ref, inv_ref, dq_ref, dk_ref, dv_ref, probs_s, terms_s
):
    step = pl.program_id(0)
    width = dq_ref.shape[1]
    keys = v_ref.shape[1]
    size = chunks(keys)

    @pl.when(step == 0)
    def _():
        dk_ref[...] = jnp.zeros_like(dk_ref)
        dv_ref[...] = jnp.zeros_like(dv_ref)

    query = qa_ref[...]
    d_out = do_ref[...]
    inverse = inv_ref[...]

    def first(chunk, delta):
        at = pl.ds(pl.multiple_of(chunk * size, 128), size)
        scores = lax.dot_general(
            ka_ref[:, at], query, (((0,), (0,)), ((), ())), preferred_element_type=jnp.float32
        )
        probs = jnp.exp(scores) * inverse
        d_probs = lax.dot_general(
            v_ref[:, at], d_out, (((0,), (0,)), ((), ())), preferred_element_type=jnp.float32
        )
        terms = probs * d_probs
        probs_s[at, :] = probs
        terms_s[at, :] = terms
        return delta + jnp.sum(terms, 0, keepdims=True)

    limit = limit_ref[step]
    delta = lax.fori_loop(0, limit, first, jnp.zeros((1, width), jnp.float32))

    def second(chunk, d_query):
        at = pl.ds(pl.multiple_of(chunk * size, 128), size)
        probs = probs_s[at, :]
        d_scores = (terms_s[at, :] - probs * delta).astype(jnp.bfloat16)
        rows = (((1,), (1,)), ((), ()))
        dk_ref[:, at] += lax.dot_general(query[:HD], d_scores, rows, preferred_element_type=jnp.float32)
        dv_ref[:, at] += lax.dot_general(
            d_out, probs.astype(jnp.bfloat16), rows, preferred_element_type=jnp.float32
        )
        return d_query + jnp.dot(ka_ref[:HD, at], d_scores, preferred_element_type=jnp.float32)

    dq_ref[...] = lax.fori_loop(0, limit, second, jnp.zeros((HD, width), jnp.float32))


def attend_backward(qa, ka, everyone, d_out, inverse, limits):
    queries, keys = qa.shape[1], ka.shape[1]
    width = query_width(keys)

    def part(rows):
        return pl.BlockSpec((rows, width), lambda step: (0, step))

    return pl.pallas_call(
        backward_kernel,
        grid=(queries // width,),
        out_shape=(
            jax.ShapeDtypeStruct((HD, queries), jnp.float32),
            jax.ShapeDtypeStruct((HD, keys), jnp.float32),
            jax.ShapeDtypeStruct((HD, keys), jnp.float32),
        ),
        in_specs=[
            pl.BlockSpec(memory_space=pltpu.SMEM),
            part(qa.shape[0]),
            whole(ka.shape),
            kind_block(everyone, 2),
            part(HD),
            part(1),
        ],
        out_specs=(part(HD), whole((HD, keys)), whole((HD, keys))),
        scratch_shapes=[
            pltpu.VMEM((keys, width), jnp.float32),
            pltpu.VMEM((keys, width), jnp.float32),
        ],
        compiler_params=pltpu.CompilerParams(
            vmem_limit_bytes=room(
                *(((ka.shape[0], count), jnp.bfloat16) for count in (queries, keys) * 4),
                *(((keys, width), jnp.float32),) * 2,
                ((4 * HD, keys), jnp.float32),
            )
        ),
        name="attend_backward",
    )(limits, qa, ka, everyone, d_out, inverse)


def layer_mod(resid, shift, scale):
    centered = resid - jnp.mean(resid, -1, keepdims=True)
    normed = centered * lax.rsqrt(jnp.mean(centered * centered, -1, keepdims=True) + 1e-06)
    return normed * (1.0 + scale) + shift


def low(value):
    return lax.reduce_precision(value, 8, 7)


def norm_factor(value, axis):
    return lax.rsqrt(jnp.mean(value * value, axis, keepdims=True) + 1e-06)


def unit_back(grad, unit, factor):
    return factor * (grad - unit * jnp.mean(unit * grad, 0, keepdims=True))


def gelu_tanh(value):
    return jax.nn.gelu(value, approximate=True)


def contract(left, right, left_dim, right_dim):
    return lax.dot_general(
        left, right, (((left_dim,), (right_dim,)), ((), ())), preferred_element_type=jnp.float32
    )


def adamw(weight, first, second, grad, rate):
    first = 0.5 * first + 0.5 * grad
    second = 0.5 * second + 0.5 * grad * grad
    fix = 1.0 - 0.5**STEP
    update = first / fix / (jnp.sqrt(second / fix) + 1e-08)
    return (first, second, weight - rate * (update + 0.05 * weight))


def pick(value, index):
    return lax.dynamic_index_in_dim(value, index, 0, keepdims=False)


def per_device(
    codes,
    targets,
    tok_weights,
    group_ids,
    labels,
    tables_w,
    tables_m,
    tables_v,
    ada_w,
    ada_m,
    ada_v,
    attn_w,
    attn_m,
    attn_v,
    mlp_w,
    mlp_m,
    mlp_v,
    head_w,
    head_m,
    head_v,
    small_w,
    small_m,
    small_v,
):
    sizes = {axis: lax.axis_size(axis) for axis in AXES}
    seq = sizes["seq"]
    at_seq, at_tp, at_dp = (lax.axis_index(axis) for axis in AXES)
    bf16, f32 = jnp.bfloat16, jnp.float32
    tokens = codes.shape[1]
    block = tokens // 2
    width = ada_w.shape[1] // 8
    rows_own = tables_w.shape[1]
    owners = seq * 2
    rows, items = labels.shape
    quarter = head_w.shape[1] // 2
    head_cols = small_w.shape[1] // 2
    heads = head_cols // HD
    pairs = rows * heads

    def quarters(*weights):
        mine, other = [], []
        for value in weights:
            halves = value.astype(bf16).reshape(rows_own, 2, -1)
            mine.append(lax.dynamic_index_in_dim(halves, at_dp, 1, keepdims=False))
            other.append(lax.dynamic_index_in_dim(halves, 1 - at_dp, 1, keepdims=False))
        mine = jnp.concatenate(mine, 1)
        got = swapped(jnp.concatenate(other, 1), "dp")
        return jnp.where(
            at_dp == 0, jnp.concatenate([mine, got], 0), jnp.concatenate([got, mine], 0)
        )

    def everywhere(block):
        return lax.all_gather(block, "seq", axis=0, tiled=True)

    attn_block = quarters(attn_w[0], attn_w[1], attn_w[2], attn_w[3])
    codes, attn_block = lax.optimization_barrier((codes, attn_block))
    attn_all = everywhere(attn_block)
    w_qkv, w_out = jnp.split(attn_all, [3 * head_cols], 1)
    rest_block = quarters(mlp_w[0], mlp_w[1], head_w)
    codes, rest_block = lax.optimization_barrier((codes, rest_block))
    mlp_block, head_block = jnp.split(rest_block, [2 * quarter], 1)
    w_up, w_down = jnp.split(everywhere(mlp_block), 2, 1)
    w_head = everywhere(head_block)

    label_flat = labels.reshape(-1)
    class_ids = lax.broadcasted_iota(jnp.int32, (NCLS, 1), 0)
    classes = tables_w[V : V + NCLS].astype(bf16)
    cond_own = contract((class_ids == label_flat[None, :]).astype(bf16), classes, 0, 0)
    silu_own = low(jax.nn.silu(cond_own))
    ada = low(ada_w)
    mods_part = contract(silu_own.astype(bf16), ada.astype(bf16), 1, 0)
    mods_part = jnp.transpose(mods_part.reshape(rows * items, owners, -1), (1, 0, 2))

    groups_chunk = lax.dynamic_slice_in_dim(group_ids[0], at_seq * tokens, tokens)
    ints = jnp.stack([codes[0], targets[0], tok_weights[0], groups_chunk])
    levels = low(tables_w[V + NCLS :])
    slot = rows * items * (8 * width // owners)
    shared = [ints.astype(f32).reshape(-1), levels.reshape(-1)]
    extra = sum(value.size for value in shared)
    shared.append(jnp.zeros((-(slot + extra) % 1024,), f32))
    shared = jnp.broadcast_to(jnp.concatenate(shared)[None], (owners, (slot + extra + 1023) // 1024 * 1024 - slot))
    opening = jnp.concatenate([mods_part.reshape(owners, -1), shared], 1).reshape(owners, 8, -1)
    (opening,) = direct([(opening, True)], ("seq", "dp"), sizes, 1)
    opening = opening.reshape(owners, -1)
    mods_sum = opening[:, :slot].reshape(mods_part.shape)
    ints_all = opening[:, slot : slot + ints.size].astype(jnp.int32)
    levels = opening[:, slot + ints.size : slot + extra].reshape(owners, LEVELS, rows_own)
    levels = jnp.pad(levels.astype(bf16), ((0, 0), (0, 16 - LEVELS), (0, 0)))
    levels = jnp.transpose(levels, (1, 0, 2)).reshape(16, width)
    ints_all = ints_all.reshape(seq, rows, 4, tokens)
    own_ints = pick(ints_all, at_seq).reshape(rows, 4, 2, block)
    own_ints = jnp.where(at_dp == 0, own_ints, own_ints[::-1])
    own_ints = jnp.where(at_tp == 0, own_ints, own_ints[:, :, ::-1])
    own_ints = jnp.transpose(own_ints, (1, 0, 2, 3)).reshape(4, rows * tokens)
    weight_total = jnp.sum(ints_all[:, :, 2]).astype(f32)

    half_ints = ints_all.reshape(seq, rows, 4, 2, block)
    half_ints = lax.dynamic_index_in_dim(half_ints, at_tp, 3, keepdims=False)

    def one_hot(index, count):
        return (lax.broadcasted_iota(jnp.int32, (count, 1), 0) == index[None, :]).astype(bf16)

    looked = contract(tables_w[:V].astype(bf16), one_hot(half_ints[:, :, 0].reshape(-1), V), 0, 0).astype(bf16)
    looked = jnp.transpose(looked.reshape(rows_own, owners, block), (1, 0, 2))
    resid, mods_all = direct(
        [(looked, True), (jnp.sum(mods_sum, 0), False)], ("seq", "dp"), sizes, 2
    )
    level_of = own_ints[3, :block] % LEVELS
    resid = resid.reshape(width, block).T.astype(f32) + contract(one_hot(level_of, 16), levels, 0, 0)
    mods_all = jnp.transpose(mods_all, (1, 0, 2)).reshape(rows, items, 8, width)
    mods_own = pick(mods_all, at_dp)
    item_of = own_ints[3, :block] // LEVELS
    select = (item_of[:, None] == jnp.arange(items)[None, :]).astype(f32)

    def mod(part):
        return sum(select[:, i : i + 1] * mods_own[i, part][None, :] for i in range(items))

    mods_rows = mods_own.reshape(items * 8, width)
    select_lanes = jnp.pad(select, ((0, 0), (0, 128 - items)))

    def run_stage(mode, parts, terms, values, sums, number):
        return stage(
            mode, parts, items, sizes, terms, values, mods_rows, select_lanes, sums, number
        )

    both = ints_all.reshape(owners, 4, 2, block)
    both = jnp.where(at_tp == 0, both, both[:, :, ::-1])
    ids = [
        kind(both[:, index, side]).reshape(1, -1)
        for side in range(2)
        for index, kind in ((0, lambda value: value), (3, lambda value: value % LEVELS))
    ]
    h_one = group_gather(layer_mod(resid, mod(0), mod(1)).astype(bf16))
    qkv = contract(w_qkv, h_one, 0, 1).reshape(3, heads, HD, rows * tokens)
    bias = lax.dynamic_slice_in_dim(small_w, at_dp * head_cols, head_cols, 1)
    bias = bias.reshape(2, heads, HD, 1)
    q_raw, k_raw, v_raw = qkv[0] + bias[0], qkv[1], qkv[2] + bias[1]
    q_factor, k_factor = norm_factor(q_raw, 1), norm_factor(k_raw, 1)
    units = jnp.stack([q_raw * q_factor * 0.25, k_raw * k_factor, v_raw]).astype(bf16)
    factors = jnp.zeros((heads, 6, rows * tokens), f32)
    factors = jnp.concatenate([q_factor, k_factor, factors], 1)[None]
    pair_own, pair_factors = pair_exchange([units, factors], sizes, heads, tokens, True, 3)
    pair = at_seq % pairs
    row_groups = lax.dynamic_index_in_dim(ints_all[:, :, 3], pair // heads, 1, keepdims=False).reshape(1, -1)
    turns = seq // pairs
    same_pair = [[turn * pairs + index for turn in range(turns)] for index in range(pairs)]

    def own_keys(value):
        if turns == 1:
            return value
        return lax.psum_scatter(
            value, "seq", scatter_dimension=1, tiled=True, axis_index_groups=same_pair
        )

    pair_all = pair_own
    if turns > 1:
        pair_all = lax.all_gather(
            pair_own, "seq", axis=2, tiled=True, axis_index_groups=same_pair
        )
    query_groups = lax.dynamic_slice_in_dim(
        row_groups, at_seq // pairs * pairs * tokens, pairs * tokens, 1
    )
    query_groups = jnp.concatenate([query_groups, query_groups // LEVELS * LEVELS])
    extra = -(-items * LEVELS // 16) * 16
    key_levels = row_groups[0] % LEVELS
    top_levels = jnp.max((query_groups[0] % LEVELS).reshape(-1, query_width(seq * tokens)), 1)
    places = jnp.arange(1, seq * tokens + 1)
    reach = jnp.max(jnp.where(key_levels[None, :] <= top_levels[:, None], places[None, :], 0), 1)
    size = chunks(seq * tokens)
    limits = (reach + size - 1) // size
    out_pair, inverse, qa, ka = attend_forward(
        pair_own, pair_all, query_groups, row_groups, extra, limits
    )
    (heads_out,) = pair_exchange([out_pair[None]], sizes, heads, tokens, False, 4)
    heads_out = heads_out.reshape(head_cols, rows * tokens)
    attn_out, x_one, h_two = run_stage(
        "forward", (2, 3, 4), contract(heads_out, w_out, 0, 1), [resid], [], 10
    )
    up_val = contract(h_two, w_up, 1, 0)
    act = gelu_tanh(up_val).astype(bf16)
    mlp_out, x_two, h_three = run_stage(
        "forward", (5, 6, 7), contract(act, w_down, 1, 1), [x_one], [], 11
    )
    logits = contract(h_three, w_head, 1, 0)

    first_code = (at_tp * 2 + at_dp) * quarter
    hit = (own_ints[1][:, None] - first_code == jnp.arange(quarter)[None, :]).astype(f32)
    local_top = jnp.max(logits, 1)
    local_sum = jnp.sum(jnp.exp(logits - local_top[:, None]), 1)
    linear_part = 0.9 * jnp.sum(hit * logits, 1) + 0.1 / V * jnp.sum(logits, 1)
    stats = jnp.stack([local_top, local_sum, linear_part]).reshape(3, rows, 2, block)

    def stats_joined(one, two):
        top = jnp.maximum(one[0], two[0])
        total = one[1] * jnp.exp(one[0] - top) + two[1] * jnp.exp(two[0] - top)
        return jnp.stack([top, total, one[2] + two[2]])

    stats = stats_joined(stats, swapped(stats, "dp")[:, ::-1])
    stats = stats_joined(stats, swapped(stats, "tp")[:, :, ::-1])
    stats = stats.reshape(3, rows * tokens)
    log_total = stats[0] + jnp.log(stats[1])
    weights = own_ints[2].astype(f32)
    loss_part = jnp.sum((weights * (log_total - stats[2]))[:block])
    scale_rows = 128.0 * weights / weight_total
    probs = jnp.exp(logits - log_total[:, None])
    d_logits = (scale_rows[:, None] * (probs - 0.9 * hit - 0.1 / V)).astype(bf16)

    def scattered(value):
        return lax.psum_scatter(value, "seq", scatter_dimension=0, tiled=True).astype(f32)

    def by_place(value):
        return value.reshape(seq // 2, 2, 2 * rows_own, -1)

    d_h_three = contract(d_logits, w_head, 1, 1)
    cuts = [0, quarter * 4 // 8, quarter]
    head_parts = [
        by_place(contract(h_three, d_logits[:, first:last], 0, 0))
        for first, last in zip(cuts, cuts[1:])
    ]
    d_x_two, sums_three, d_mlp, grad_head_one = run_stage(
        "backward", (7, 5), d_h_three, [x_two, mlp_out], head_parts[:1], 12
    )
    d_act = contract(d_mlp, w_down, 1, 0)
    d_up = jax.vjp(gelu_tanh, up_val)[1](d_act)[0].astype(bf16)
    grad_mlp = outer([(h_two, d_up, 0), (d_mlp, act, 0)], bf16)
    grad_mlp, d_up = lax.optimization_barrier((grad_mlp, d_up))
    grad_mlp = scattered(grad_mlp)
    d_h_two = contract(d_up, w_up, 1, 1)
    d_x_one, sums_two, d_attn = run_stage(
        "backward", (4, 2), d_h_two, [x_one, attn_out, d_x_two], [], 13
    )
    d_heads = contract(w_out, d_attn, 0, 1).astype(bf16).reshape(1, heads, HD, rows * tokens)
    (d_out_pair,) = pair_exchange([d_heads], sizes, heads, tokens, True, 5)
    d_query, d_keys, d_values = attend_backward(qa, ka, pair_all, d_out_pair[0], inverse, limits)
    q_factor, k_factor = pair_factors[0, 0:1], pair_factors[0, 1:2]
    d_q = unit_back(d_query, pair_own[0].astype(f32) * 4.0, q_factor) * 0.25
    d_k = unit_back(own_keys(d_keys), pair_own[1].astype(f32), k_factor)
    stacked = jnp.stack([d_q, d_k, own_keys(d_values)]).astype(bf16)
    (d_qkv,) = pair_exchange([stacked], sizes, heads, tokens, False, 6)
    d_qkv = d_qkv.reshape(3 * head_cols, rows * tokens)
    grad_attn = outer([(h_one, d_qkv, 1), (d_attn, heads_out, 1)], f32)
    bias_sums = jnp.sum(d_qkv.astype(f32), 1).reshape(3, head_cols)[::2]
    d_resid, sums_one, grad_head_two = run_stage(
        "last",
        (1,),
        contract(d_qkv, w_qkv, 0, 1),
        [resid, d_x_one],
        head_parts[1:],
        14,
    )

    gate = 2 * items
    d_mods = jnp.concatenate(
        [sums_one, sums_two[gate:], sums_two[:gate], sums_three[gate:], sums_three[:gate]], 0
    )
    d_mods = d_mods.reshape(8, items, owners // 8, -1)
    d_mods = jnp.transpose(d_mods, (0, 2, 1, 3)).reshape(owners, items, -1)
    d_cols = d_resid.T.reshape(owners, rows_own, block)
    slot = d_mods.shape[2]
    bias_row = jnp.pad(bias_sums.reshape(-1), (0, -bias_sums.size % slot)).reshape(-1, slot)
    d_mods = jnp.concatenate([d_mods, jnp.broadcast_to(bias_row, (owners,) + bias_row.shape)], 1)
    d_mods, d_mods_in, grad_attn, g_codes, g_levels = tail_stage(
        d_cols, d_mods, items, by_place(grad_attn), ids, sizes, 8
    )
    bias_sums = d_mods_in[:, items:].reshape(owners, -1)[:, : 2 * head_cols]
    bias_sums = jnp.sum(bias_sums.reshape(seq, 2, 2, head_cols), 0)
    g_small = jnp.concatenate([bias_sums[0], bias_sums[1]], 1)
    d_mods = d_mods.reshape(owners, rows * items, -1)
    d_mods = jnp.transpose(d_mods, (1, 0, 2)).reshape(rows * items, 8 * width)
    g_ada = sum(silu_own[i][:, None] * d_mods[i][None, :] for i in range(rows * items))
    d_silu = jnp.stack([jnp.sum(ada * d_mods[i][None, :], 1) for i in range(rows * items)])
    d_cond = jax.vjp(jax.nn.silu, cond_own)[1](d_silu)[0]

    class_lanes = lax.broadcasted_iota(jnp.int32, (1, NCLS), 1)
    g_classes = sum(
        jnp.where(class_lanes == label_flat[i], d_cond[i][:, None], 0.0) for i in range(rows * items)
    )
    g_tables = jnp.concatenate([g_codes, g_classes, g_levels[:, :LEVELS]], 1).T

    def owned(value):
        parts = value.reshape(2, rows_own, -1)
        mine = pick(parts, at_dp)
        return mine, swapped(pick(parts, 1 - at_dp), "dp")

    def joined(pair, first, count):
        mine, got = (part[:, first : first + count] for part in pair)
        return jnp.where(
            at_dp == 0, jnp.concatenate([mine, got], 1), jnp.concatenate([got, mine], 1)
        )

    def side_by_side(value, first, count):
        other = value.shape[1] // 2 + first
        return [value[:, first : first + count], value[:, other : other + count]]

    g_attn = jnp.stack(
        [
            jnp.concatenate(side_by_side(grad_attn, kind * head_cols, head_cols), 1)
            for kind in range(4)
        ]
    )
    mlp_pair = owned(grad_mlp)
    g_mlp = jnp.stack([joined(mlp_pair, kind * quarter, quarter) for kind in range(2)])
    one, two = (
        side_by_side(value, 0, value.shape[1] // 2) for value in (grad_head_one, grad_head_two)
    )
    g_head = jnp.concatenate([one[0], two[0], one[1], two[1]], 1)

    local_squares = (jnp.sum(g_tables * g_tables) + jnp.sum(g_ada * g_ada)) / 2
    local_squares = (
        local_squares
        + sum(
            jnp.sum(value * value)
            for value in (grad_attn, grad_mlp, grad_head_one, grad_head_two)
        )
    )
    local_squares = local_squares + jnp.sum(g_small * g_small) / owners
    column = lax.broadcasted_iota(jnp.int32, (8, 128), 1)
    scalars = jnp.where(column == 0, local_squares, jnp.where(column == 1, loss_part, 0.0))
    scalars = jnp.sum(direct([(scalars, False)], AXES, sizes, 9)[0], 0)
    grad_norm = jnp.sqrt(scalars[0, 0])
    loss = 128.0 * scalars[0, 1] / weight_total
    factor = jnp.minimum(1.0, 1.0 / (grad_norm + 1e-06))
    tables_n = adamw(tables_w, tables_m, tables_v, g_tables * factor, 0.3)
    ada_n = adamw(ada_w, ada_m, ada_v, g_ada * factor, 0.03)
    attn_n = adamw(attn_w, attn_m, attn_v, g_attn * factor, 0.1)
    mlp_n = adamw(mlp_w, mlp_m, mlp_v, g_mlp * factor, 0.02)
    head_n = adamw(head_w, head_m, head_v, g_head * factor, 0.03)
    small_n = adamw(small_w, small_m, small_v, g_small * factor, 0.5)
    return (
        loss,
        grad_norm,
        *tables_n,
        *ada_n,
        *attn_n,
        attn_n[2].astype(bf16),
        *mlp_n,
        mlp_n[2].astype(bf16),
        *head_n,
        head_n[2].astype(bf16),
        *small_n,
    )


def solution(mesh):
    tokens, whole_rows = P("dp", "seq"), P("dp", None)
    tables, ada = P(None, ("seq", "dp")), P(("seq", "dp"), None)
    layer, head, small = P(None, ("seq", "dp"), "tp"), P(("seq", "dp"), "tp"), P(None, "tp")
    return jax.shard_map(
        per_device,
        mesh=mesh,
        in_specs=(
            (tokens,) * 3
            + (whole_rows, P())
            + (tables,) * 3
            + (ada,) * 3
            + (layer,) * 6
            + (head,) * 3
            + (small,) * 3
        ),
        out_specs=(
            (P(), P())
            + (tables,) * 3
            + (ada,) * 3
            + (layer,) * 8
            + (head,) * 4
            + (small,) * 3
        ),
        check_vma=False,
    )
```

```python
import functools
import math

import jax
import jax.numpy as jnp
from jax import lax
from jax.experimental import pallas as pl
from jax.experimental.pallas import tpu as pltpu
from jax.sharding import PartitionSpec as P

HD = 64
V = 4096
NCLS = 1000
LEVELS = 10
STEP = 3
AXES = ("seq", "tp", "dp")
BLOCKED = -30000.0


def place(axes, sizes, index):
    coords = {axis: lax.axis_index(axis) for axis in AXES}
    for axis in reversed(axes):
        coords[axis] = lax.rem(index, sizes[axis])
        index = index // sizes[axis]
    return tuple(coords[axis] for axis in AXES)


def linear(axes, sizes):
    index = 0
    for axis in axes:
        index = index * sizes[axis] + lax.axis_index(axis)
    return index


def direct_kernel(axes, sizes, spreads, *refs):
    count = math.prod(sizes[axis] for axis in axes)
    number = len(spreads)
    sources, targets = refs[:number], refs[number : 2 * number]
    send, recv, own = refs[2 * number :]
    me = linear(axes, sizes)
    barrier = pltpu.get_barrier_semaphore()

    def peer_at(step):
        return lax.rem(me + step, count)

    def greet(step, carry):
        pl.semaphore_signal(
            barrier,
            inc=1,
            device_id=place(axes, sizes, peer_at(step)),
            device_id_type=pl.DeviceIdType.MESH,
        )
        return carry

    lax.fori_loop(1, count, greet, 0)
    pl.semaphore_wait(barrier, count - 1)

    def ends(index, peer):
        source = sources[index].at[peer] if spreads[index] else sources[index]
        return source, targets[index].at[me]

    def copy_at(step, index):
        peer = peer_at(step)
        source, target = ends(index, peer)
        return pltpu.make_async_remote_copy(
            src_ref=source,
            dst_ref=target,
            send_sem=send.at[index, step],
            recv_sem=recv.at[index, step],
            device_id=place(axes, sizes, peer),
            device_id_type=pl.DeviceIdType.MESH,
        )

    def start(step, carry):
        for index in range(number):
            copy_at(step, index).start()
        return carry

    def finish(step, carry):
        for index in range(number):
            copy_at(step, index).wait()
        return carry

    lax.fori_loop(1, count, start, 0)
    local = []
    for index in range(number):
        source, target = ends(index, me)
        local.append(pltpu.make_async_copy(source, target, own.at[index]))
        local[-1].start()
    lax.fori_loop(1, count, finish, 0)
    for copy in local:
        copy.wait()


def direct(payloads, axes, sizes, number):
    count = math.prod(sizes[axis] for axis in axes)
    values = [value for value, _ in payloads]
    spreads = tuple(spread for _, spread in payloads)
    shapes = [
        jax.ShapeDtypeStruct(value.shape if spread else (count,) + value.shape, value.dtype)
        for value, spread in payloads
    ]
    return pl.pallas_call(
        functools.partial(direct_kernel, axes, sizes, spreads),
        out_shape=shapes,
        in_specs=[pl.BlockSpec(memory_space=pl.ANY)] * len(values),
        out_specs=[pl.BlockSpec(memory_space=pl.ANY)] * len(values),
        scratch_shapes=[
            pltpu.SemaphoreType.DMA((len(values), count)),
            pltpu.SemaphoreType.DMA((len(values), count)),
            pltpu.SemaphoreType.DMA((len(values),)),
        ],
        compiler_params=pltpu.CompilerParams(collective_id=number, has_side_effects=True),
        name=f"direct_{number}",
    )(*values)


def pairs_kernel(sizes, heads, tokens, outward, count, *refs):
    sources, targets = refs[:count], refs[count : 2 * count]
    send, recv, own = refs[2 * count :]
    pairs = 2 * heads
    half = tokens // 2
    at_seq, at_tp, at_dp = (lax.axis_index(axis) for axis in AXES)
    base = at_seq // pairs * pairs
    me = lax.rem(at_seq, pairs)

    def device(peer):
        return (base + peer, at_tp, at_dp)

    barrier = pltpu.get_barrier_semaphore()
    for step in range(1, pairs):
        pl.semaphore_signal(
            barrier,
            inc=1,
            device_id=device(lax.rem(me + step, pairs)),
            device_id_type=pl.DeviceIdType.MESH,
        )
    pl.semaphore_wait(barrier, pairs - 1)

    def ends(index, piece, pair, chunk):
        row = lax.rem(pair // heads + at_dp, 2)
        inner = pl.ds(pl.multiple_of((row * 2 + piece) * half, half), half)
        outer = pl.ds(
            pl.multiple_of(chunk * tokens + lax.rem(piece + at_tp, 2) * half, half), half
        )
        head = lax.rem(pair, heads)
        if outward:
            return sources[index].at[:, head, :, inner], targets[index].at[:, :, outer]
        return sources[index].at[:, :, outer], targets[index].at[:, head, :, inner]

    copies = []
    for step in range(1, pairs):
        peer = lax.rem(me + step, pairs)
        pair, chunk = (peer, me) if outward else (me, peer)
        for index in range(count):
            for piece in range(2):
                source, target = ends(index, piece, pair, chunk)
                copies.append(
                    pltpu.make_async_remote_copy(
                        src_ref=source,
                        dst_ref=target,
                        send_sem=send.at[index, piece, step],
                        recv_sem=recv.at[index, piece, step],
                        device_id=device(peer),
                        device_id_type=pl.DeviceIdType.MESH,
                    )
                )
                copies[-1].start()
    for index in range(count):
        for piece in range(2):
            source, target = ends(index, piece, me, me)
            copies.append(pltpu.make_async_copy(source, target, own.at[index, piece]))
            copies[-1].start()
    for copy in copies:
        copy.wait()


def pair_exchange(values, sizes, heads, tokens, outward, number):
    pairs = 2 * heads
    if outward:
        shapes = [(v.shape[0], v.shape[2], pairs * tokens) for v in values]
    else:
        shapes = [(v.shape[0], heads, v.shape[1], 2 * tokens) for v in values]
    count = len(values)
    return pl.pallas_call(
        functools.partial(pairs_kernel, sizes, heads, tokens, outward, count),
        out_shape=[jax.ShapeDtypeStruct(s, v.dtype) for s, v in zip(shapes, values)],
        in_specs=[pl.BlockSpec(memory_space=pl.ANY)] * count,
        out_specs=[pl.BlockSpec(memory_space=pl.ANY)] * count,
        scratch_shapes=[
            pltpu.SemaphoreType.DMA((count, 2, pairs)),
            pltpu.SemaphoreType.DMA((count, 2, pairs)),
            pltpu.SemaphoreType.DMA((count, 2)),
        ],
        compiler_params=pltpu.CompilerParams(collective_id=number, has_side_effects=True),
        name=f"pairs_{number}",
    )(*values)


def swapped(value, axis):
    return lax.ppermute(value, axis, [(0, 1), (1, 0)])


def group_gather(value):
    row = jnp.concatenate([value, swapped(value, "tp")], 0)
    return jnp.concatenate([row, swapped(row, "dp")], 0)


def remote(source, target, send, recv, device):
    return pltpu.make_async_remote_copy(
        src_ref=source,
        dst_ref=target,
        send_sem=send,
        recv_sem=recv,
        device_id=device,
        device_id_type=pl.DeviceIdType.MESH,
    )


def reduce_steps(x, out, scratch, sizes):
    from_y, staged, from_low, from_high, b_staged, b_low, b_high, b_y, total, send, recv = scratch
    deep = sizes["seq"] // 2
    at_seq, at_tp, at_dp = (lax.axis_index(axis) for axis in AXES)
    z, y = at_seq // 2, lax.rem(at_seq, 2)
    beside = (at_seq + 1 - 2 * y, at_tp, at_dp)
    above = (lax.min(at_seq + 2, sizes["seq"] - 1), at_tp, at_dp)
    below = (lax.max(at_seq - 2, 0), at_tp, at_dp)
    split = from_y.shape[2]
    first, second = pl.ds(0, split), pl.ds(split, x.shape[3] - split)

    def block(index):
        return lax.rem(z + index, deep)

    def copy(kind, slot, source, target, device):
        return remote(source, target, send.at[kind, slot], recv.at[kind, slot], device)

    def y_copy(index):
        return copy(0, index, x.at[block(index), 1 - y, :, first], from_y.at[index], beside)

    def up_copy(turn):
        return copy(1, turn - 1, staged.at[deep - turn], from_low.at[turn - 1], above)

    def down_copy(turn):
        return copy(2, turn - 1, staged.at[turn], from_high.at[turn - 1], below)

    def b_up_copy(turn):
        return copy(3, turn - 1, b_staged.at[deep - turn], b_low.at[turn - 1], above)

    def b_down_copy(turn):
        return copy(4, turn - 1, b_staged.at[turn], b_high.at[turn - 1], below)

    def b_y_copy():
        return copy(5, 0, b_staged.at[0, 1 - y], b_y, beside)

    def goes_up(turn):
        return (z <= turn - 1) & (z < deep - 1)

    def goes_down(turn):
        return (z >= deep - turn) & (z > 0)

    def move(turn, went, index, there, arrived, received, started, b):
        @pl.when(went)
        def _():
            if b:
                b_staged[index] = x[block(index), :, :, second]
            else:
                y_copy(index).wait_recv()
                staged[index] = x[block(index), y, :, first] + from_y[index]
            if turn > 1:

                @pl.when(there)
                def _():
                    arrived(turn - 1).wait_recv()
                    if b:
                        b_staged[index] += received[turn - 2]
                    else:
                        staged[index] += received[turn - 2]

            started(turn).start()

    def main(turn):
        move(turn, goes_up(turn), deep - turn, z > 0, up_copy, from_low, up_copy, False)
        move(turn, goes_down(turn), turn, z < deep - 1, down_copy, from_high, down_copy, False)

    def rest(turn):
        move(turn, goes_up(turn), deep - turn, z > 0, b_up_copy, b_low, b_up_copy, True)
        move(turn, goes_down(turn), turn, z < deep - 1, b_down_copy, b_high, b_down_copy, True)

    def begin():
        for turn in range(deep - 1):
            y_copy(lax.select(z < deep // 2, deep - 1 - turn, turn + 1)).start()
        y_copy(0).start()
        rest(1)

    def rest_end():
        b_staged[0] = x[z, :, :, second]

        @pl.when(z > 0)
        def _():
            b_up_copy(deep - 1).wait_recv()
            b_staged[0] += b_low[deep - 2]

        @pl.when(z < deep - 1)
        def _():
            b_down_copy(deep - 1).wait_recv()
            b_staged[0] += b_high[deep - 2]

        b_y_copy().start()

    def middle(turn):
        main(turn)
        if turn < deep - 1:
            rest(turn + 1)
        else:
            rest_end()

    columns = x.shape[3]
    half = total.shape[0] // 2
    place_in = pl.ds(pl.multiple_of(at_dp * columns, 128), columns)

    def core_copy():
        given = total.at[pl.ds(pl.multiple_of((1 - at_dp) * half, half), half)]
        return copy(5, 1, given, out.at[:, place_in], (at_seq, at_tp, 1 - at_dp))

    def main_end():
        y_copy(0).wait_recv()
        total[:, first] = x[z, y, :, first] + from_y[0]

        @pl.when(z > 0)
        def _():
            up_copy(deep - 1).wait_recv()
            total[:, first] += from_low[deep - 2]

        @pl.when(z < deep - 1)
        def _():
            down_copy(deep - 1).wait_recv()
            total[:, first] += from_high[deep - 2]

    def finish():
        b_y_copy().wait_recv()
        total[:, second] = b_staged[0, y] + b_y[...]
        core_copy().start()
        out[:, place_in] = total[pl.ds(pl.multiple_of(at_dp * half, half), half), :]
        core_copy().wait()
        for index in range(deep):
            y_copy(index).wait_send()
        b_y_copy().wait_send()
        for turn in range(1, deep):

            @pl.when(goes_up(turn))
            def _():
                up_copy(turn).wait_send()
                b_up_copy(turn).wait_send()

            @pl.when(goes_down(turn))
            def _():
                down_copy(turn).wait_send()
                b_down_copy(turn).wait_send()

    turns = [functools.partial(middle, turn) for turn in range(1, deep)]
    return [begin] + turns + [main_end, finish]


def reduce_scratch(value):
    deep, _, rows, columns = value.shape
    split = max(128, columns * 3 // 4 // 128 * 128)
    rest = columns - split
    kind = value.dtype
    return [
        pltpu.VMEM((deep, rows, split), kind),
        pltpu.VMEM((deep, rows, split), kind),
        pltpu.VMEM((deep - 1, rows, split), kind),
        pltpu.VMEM((deep - 1, rows, split), kind),
        pltpu.VMEM((deep, 2, rows, rest), kind),
        pltpu.VMEM((deep - 1, 2, rows, rest), kind),
        pltpu.VMEM((deep - 1, 2, rows, rest), kind),
        pltpu.VMEM((rows, rest), kind),
        pltpu.VMEM((rows, columns), kind),
        pltpu.SemaphoreType.DMA((6, deep)),
        pltpu.SemaphoreType.DMA((6, deep)),
    ]


def reduced(value):
    rows, columns = value.shape[2:]
    return jax.ShapeDtypeStruct((rows // 2, 2 * columns), value.dtype)


def room(*shapes):
    size = 0
    for shape, kind in shapes:
        padded = list(shape)
        padded[-1] = -(-padded[-1] // 128) * 128
        if len(padded) > 1:
            padded[-2] = -(-padded[-2] // 16) * 16
        size += math.prod(padded) * jnp.dtype(kind).itemsize
    return min(size + 6 * 1024 * 1024, 60 * 1024 * 1024)


def sizes_of(scratch):
    return [(item.shape, item.dtype) for item in scratch if item.memory_space == pltpu.VMEM]


PIECES = 4


def normed_of(x):
    centered = x - jnp.mean(x, -1, keepdims=True)
    factor = lax.rsqrt(jnp.mean(centered * centered, -1, keepdims=True) + 1e-06)
    return centered * factor, factor


def stage_kernel(mode, parts, items, sizes, given, jobs, *refs):
    refs = list(refs)

    def take(count):
        taken, refs[:count] = refs[:count], []
        return taken

    terms, *values = take(given)
    mods, select = take(2)
    sums_in = take(jobs)
    gathers = mode != "last"
    first_out, second_out = take(2)
    gathered = take(1)[0] if gathers else None
    sums_out = take(jobs)
    from_core, passed, from_x, send, recv = take(5)
    scratch = [take(11) for _ in range(jobs)]
    block = terms.shape[1]
    size = block // PIECES
    at_seq, at_tp, at_dp = (lax.axis_index(axis) for axis in AXES)
    core, across = (at_seq, at_tp, 1 - at_dp), (at_seq, 1 - at_tp, at_dp)

    barrier = pltpu.get_barrier_semaphore()

    def greet(device):
        pl.semaphore_signal(barrier, inc=1, device_id=device, device_id_type=pl.DeviceIdType.MESH)

    greet(core)
    greet(across)
    expected = 2
    if jobs:
        z, y, deep = at_seq // 2, lax.rem(at_seq, 2), sizes["seq"] // 2
        greet((at_seq + 1 - 2 * y, at_tp, at_dp))

        @pl.when(z > 0)
        def _():
            greet((at_seq - 2, at_tp, at_dp))

        @pl.when(z < deep - 1)
        def _():
            greet((at_seq + 2, at_tp, at_dp))

        expected = 3 + lax.min(z, 1) + lax.min(deep - 1 - z, 1)
    pl.semaphore_wait(barrier, expected)

    def rows(piece):
        return pl.ds(piece * size, size)

    def copy(kind, piece, source, target, device):
        return remote(source, target, send.at[kind, piece], recv.at[kind, piece], device)

    def core_copy(piece):
        return copy(0, piece, terms.at[pl.ds(2, 2), rows(piece)], from_core.at[:, rows(piece)], core)

    def x_copy(piece):
        return copy(1, piece, passed.at[rows(piece)], from_x.at[rows(piece)], across)

    def share_x(piece):
        return copy(2, piece, gathered.at[0, rows(piece)], gathered.at[1, rows(piece)], across)

    def share_core(piece):
        return copy(3, piece, gathered.at[0, rows(piece)], gathered.at[2, rows(piece)], core)

    def forward_core(piece):
        return copy(4, piece, gathered.at[1, rows(piece)], gathered.at[3, rows(piece)], core)

    waiting = []
    for index in range(jobs):
        waiting.append(reduce_steps(sums_in[index], sums_out[index], scratch[index], sizes))

    def advance():
        for steps in waiting:
            if steps:
                steps.pop(0)()

    for piece in range(PIECES):
        core_copy(piece).start()
    advance()
    for piece in range(PIECES):
        at = rows(piece)
        core_copy(piece).wait_recv()
        passed[at, :] = terms[1, at, :] + from_core[1, at, :]
        x_copy(piece).start()
    for piece in range(PIECES):
        at = rows(piece)
        chosen = [select[at, i : i + 1] for i in range(items)]

        def mod(part):
            return sum(chosen[i] * mods[i * 8 + part : i * 8 + part + 1, :] for i in range(items))

        def tally(index, value):
            for i in range(items):
                slot = pl.ds(index * items + i, 1)
                part = jnp.sum(chosen[i] * value, 0, keepdims=True)
                if piece == 0:
                    second_out[slot, :] = part
                else:
                    second_out[slot, :] += part

        x_copy(piece).wait_recv()
        total = terms[0, at, :] + from_core[0, at, :] + from_x[at, :]
        if mode == "forward":
            gate, shift, scale = parts
            x = values[0][at, :] + mod(gate) * total
            first_out[at, :] = total
            second_out[at, :] = x
            result = normed_of(x)[0] * (1.0 + mod(scale)) + mod(shift)
        else:
            normed, factor = normed_of(values[0][at, :])
            grad = total * (1.0 + mod(parts[0]))
            d_x = factor * (
                grad
                - jnp.mean(grad, -1, keepdims=True)
                - normed * jnp.mean(grad * normed, -1, keepdims=True)
            )
            if given > (3 if gathers else 2):
                d_x = d_x + values[-1][at, :]
            first_out[at, :] = d_x
            tally(0, total)
            tally(1, total * normed)
            if gathers:
                tally(2, d_x * values[1][at, :])
                result = d_x * mod(parts[1])
        if gathers:
            gathered[0, at, :] = result.astype(jnp.bfloat16)
            share_x(piece).start()
            share_core(piece).start()
        advance()
    if gathers:
        for piece in range(PIECES):
            share_x(piece).wait_recv()
            forward_core(piece).start()
    while any(waiting):
        advance()
    for piece in range(PIECES):
        core_copy(piece).wait_send()
        x_copy(piece).wait_send()
        if gathers:
            share_core(piece).wait_recv()
            forward_core(piece).wait_recv()
            share_x(piece).wait_send()
            share_core(piece).wait_send()
            forward_core(piece).wait_send()


def stage(mode, parts, items, sizes, terms, values, mods, select, sums, number):
    block, width = terms.shape[0] // 4, terms.shape[1]
    f32, gathers = jnp.float32, mode != "last"
    inputs = [terms.reshape(4, block, width), *values, mods, select, *sums]
    second = {"forward": block, "backward": 3 * items, "last": 2 * items}[mode]
    shapes = [
        jax.ShapeDtypeStruct((block, width), f32),
        jax.ShapeDtypeStruct((second, width), f32),
    ]
    if gathers:
        shapes.append(jax.ShapeDtypeStruct((4, block, width), jnp.bfloat16))
    shapes += [reduced(value) for value in sums]
    scratch = [
        pltpu.VMEM((2, block, width), f32),
        pltpu.VMEM((block, width), f32),
        pltpu.VMEM((block, width), f32),
        pltpu.SemaphoreType.DMA((5, PIECES)),
        pltpu.SemaphoreType.DMA((5, PIECES)),
    ]
    for value in sums:
        scratch += reduce_scratch(value)
    results = pl.pallas_call(
        functools.partial(
            stage_kernel, mode, parts, items, sizes, 1 + len(values), len(sums)
        ),
        out_shape=shapes,
        in_specs=[pl.BlockSpec(memory_space=pltpu.VMEM)] * len(inputs),
        out_specs=[pl.BlockSpec(memory_space=pltpu.VMEM)] * len(shapes),
        scratch_shapes=scratch,
        compiler_params=pltpu.CompilerParams(
            collective_id=number,
            has_side_effects=True,
            vmem_limit_bytes=room(
                *((value.shape, value.dtype) for value in inputs + shapes), *sizes_of(scratch)
            ),
        ),
        name=f"stage_{number}",
    )(*inputs)
    outs = list(results)
    if gathers:
        outs[2] = outs[2].reshape(4 * block, width)
    return outs


def outer_kernel(dims, *refs):
    out = refs[-1]
    start = 0
    for index, dim in enumerate(dims):
        left, right = refs[2 * index], refs[2 * index + 1]
        count = right.shape[1 - dim] // 256

        def tile(step, carry, left=left, right=right, dim=dim, start=start):
            at = pl.ds(pl.multiple_of(step * 256, 256), 256)
            part = right[at, :] if dim else right[:, at]
            product = lax.dot_general(
                left[...], part, (((0,), (dim,)), ((), ())), preferred_element_type=jnp.float32
            )
            out[:, pl.ds(pl.multiple_of(start + step * 256, 256), 256)] = product.astype(out.dtype)
            return carry

        lax.fori_loop(0, count, tile, 0)
        start += count * 256


def outer(pairs, kind):
    dims = tuple(dim for _, _, dim in pairs)
    columns = sum(right.shape[1 - dim] for _, right, dim in pairs)
    inputs = [value for left, right, _ in pairs for value in (left, right)]
    rows, depth = pairs[0][0].shape[1], pairs[0][0].shape[0]
    return pl.pallas_call(
        functools.partial(outer_kernel, dims),
        out_shape=jax.ShapeDtypeStruct((rows, columns), kind),
        in_specs=[pl.BlockSpec(memory_space=pltpu.VMEM)] * len(inputs),
        out_specs=pl.BlockSpec(memory_space=pltpu.VMEM),
        cost_estimate=pl.CostEstimate(
            flops=2 * rows * columns * depth, bytes_accessed=8 * rows * columns, transcendentals=0
        ),
        compiler_params=pltpu.CompilerParams(
            vmem_limit_bytes=room(
                *((value.shape, value.dtype) for value in inputs), ((rows, columns), kind)
            )
        ),
        name="outer",
    )(*inputs)


def tail_kernel(items, sizes, *refs):
    cols, mods, x, own_codes, own_levels, other_codes, other_levels = refs[:7]
    mods_out, mods_in, sum_out, codes_out, levels_out = refs[7:12]
    own_cols, other_cols, parts, mods_own, mods_other, mods_sum = refs[12:18]
    send, recv, near, across_send, across_recv = refs[18:23]
    scratch = refs[23:]
    axes = ("seq", "dp")
    seq = sizes["seq"]
    count = seq * 2
    me = linear(axes, sizes)
    at_seq, at_tp, at_dp = (lax.axis_index(axis) for axis in AXES)
    across = (at_seq, 1 - at_tp, at_dp)
    barrier = pltpu.get_barrier_semaphore()

    def greet_device(device):
        pl.semaphore_signal(barrier, inc=1, device_id=device, device_id_type=pl.DeviceIdType.MESH)

    def greet(step, carry):
        greet_device(place(axes, sizes, lax.rem(me + step, count)))
        return carry

    lax.fori_loop(1, count, greet, 0)
    greet_device(across)
    pl.semaphore_wait(barrier, count)

    def ends(index, peer):
        if index == 0:
            return mods.at[peer], mods_in.at[me]
        if index == 1:
            return cols.at[peer], own_cols.at[me]
        return mods_sum, mods_out.at[me]

    def copy_at(index, step):
        peer = lax.rem(me + step, count)
        return remote(
            *ends(index, peer), send.at[index, step], recv.at[index, step], place(axes, sizes, peer)
        )

    def over_peers(index, action):
        def one(step, carry):
            getattr(copy_at(index, step), action)()
            return carry

        lax.fori_loop(1, count, one, 0)

    steps = reduce_steps(x, sum_out, scratch, sizes)

    def advance():
        if steps:
            steps.pop(0)()

    owners, width, block = own_cols.shape
    tokens = owners * block
    chunk = 1024
    tile = 512

    def fill(columns, side, owner):
        value = columns[owner]
        at = pl.ds(pl.multiple_of(owner * block, block), block)
        for index in range(3):
            part = value.astype(jnp.bfloat16)
            parts[side, pl.ds(index * width, width), at] = part
            value = value - part.astype(jnp.float32)

    def products(side, ids, first, height):
        def one(step, total):
            at = pl.ds(pl.multiple_of(step * chunk, chunk), chunk)
            rows = lax.broadcasted_iota(jnp.int32, (height, chunk), 0) + first
            hot = jnp.where(rows == ids[:, at], 1.0, 0.0).astype(jnp.bfloat16)
            return total + lax.dot_general(
                parts[side, :, at], hot, (((1,), (1,)), ((), ())), preferred_element_type=jnp.float32
            )

        total = jnp.zeros((3 * width, height), jnp.float32)
        total = lax.fori_loop(0, tokens // chunk, one, total)
        return total[:width] + total[width : 2 * width] + total[2 * width :]

    def tiles(side, codes, base, number):
        def one(step, carry):
            first = pl.multiple_of((base + step) * tile, tile)
            at = pl.ds(first, tile)
            value = products(side, codes, first, tile)
            if side:
                codes_out[:, at] += value
            else:
                codes_out[:, at] = value
            return carry

        lax.fori_loop(0, number, one, 0)

    def passed_on(owner):
        return remote(
            own_cols.at[owner],
            other_cols.at[owner],
            across_send.at[owner],
            across_recv.at[owner],
            across,
        )

    local = [pltpu.make_async_copy(*ends(index, me), near.at[index]) for index in range(3)]
    for index in range(2):
        over_peers(index, "start")
        local[index].start()
    over_peers(0, "wait")
    local[0].wait()
    for row in range(2):
        mine = mods_in[row, :items]
        for position in range(1, seq):
            mine = mine + mods_in[position * 2 + row, :items]
        mods_own[row] = mine
    mods_exchange = remote(
        mods_own, mods_other, across_send.at[owners], across_recv.at[owners], across
    )
    mods_exchange.start()
    local[1].wait()
    passed_on(me).start()
    fill(own_cols, 0, me)
    mods_exchange.wait()
    mods_sum[...] = mods_own[...] + mods_other[...]
    over_peers(2, "start")
    local[2].start()
    advance()

    def arrived(step, carry):
        copy_at(1, step).wait()
        owner = lax.rem(me - step + count, count)
        passed_on(owner).start()
        fill(own_cols, 0, owner)
        return carry

    lax.fori_loop(1, count, arrived, 0)
    advance()
    half = V // tile // 2
    tiles(0, own_codes, 0, half)
    advance()

    def crossed(owner, carry):
        passed_on(owner).wait()
        fill(other_cols, 1, owner)
        return carry

    lax.fori_loop(0, count, crossed, 0)
    tiles(0, own_codes, half, half)
    levels_out[...] = products(0, own_levels, 0, levels_out.shape[1])
    levels_out[...] += products(1, other_levels, 0, levels_out.shape[1])
    advance()
    tiles(1, other_codes, 0, half)
    advance()
    tiles(1, other_codes, half, half)
    while steps:
        advance()
    over_peers(2, "wait")
    local[2].wait()


def tail_stage(cols, mods, items, x, ids, sizes, number):
    count, width, block = cols.shape
    f32 = jnp.float32
    inputs = [cols, mods, x, *ids]
    in_vmem = pl.BlockSpec(memory_space=pltpu.VMEM)
    pair = (2, items, mods.shape[2])
    shapes = [
        jax.ShapeDtypeStruct((count,) + pair, f32),
        jax.ShapeDtypeStruct(mods.shape, f32),
        reduced(x),
        jax.ShapeDtypeStruct((width, V), f32),
        jax.ShapeDtypeStruct((width, 128), f32),
    ]
    scratch = [
        pltpu.VMEM(cols.shape, f32),
        pltpu.VMEM(cols.shape, f32),
        pltpu.VMEM((2, 3 * width, count * block), jnp.bfloat16),
        pltpu.VMEM(pair, f32),
        pltpu.VMEM(pair, f32),
        pltpu.VMEM(pair, f32),
        pltpu.SemaphoreType.DMA((3, count)),
        pltpu.SemaphoreType.DMA((3, count)),
        pltpu.SemaphoreType.DMA((3,)),
        pltpu.SemaphoreType.DMA((count + 1,)),
        pltpu.SemaphoreType.DMA((count + 1,)),
    ] + reduce_scratch(x)
    return pl.pallas_call(
        functools.partial(tail_kernel, items, sizes),
        out_shape=shapes,
        in_specs=[in_vmem] * len(inputs),
        out_specs=[in_vmem] * len(shapes),
        scratch_shapes=scratch,
        compiler_params=pltpu.CompilerParams(
            collective_id=number,
            has_side_effects=True,
            vmem_limit_bytes=room(
                *((value.shape, value.dtype) for value in inputs + shapes), *sizes_of(scratch)
            ),
        ),
        name=f"tail_{number}",
    )(*inputs)


def chunks(total):
    return min(total, 1024)


def forward_kernel(
    limit_ref, q_ref, k_ref, v_ref, qg_ref, kg_ref, o_ref, inv_ref, qa_ref, ka_ref, exps
):
    step = pl.program_id(0)
    width = o_ref.shape[1]
    keys = k_ref.shape[1]
    size = chunks(keys)

    @pl.when(step == 0)
    def _():
        extra = ka_ref.shape[0] - HD
        ka_ref[:HD, :] = k_ref[...]
        level = lax.broadcasted_iota(jnp.int32, (extra, keys), 0)
        ka_ref[HD:, :] = jnp.where(level == kg_ref[...], 1.0, 0.0).astype(jnp.bfloat16)
        qa_ref[:HD, :] = q_ref[...]
        level = lax.broadcasted_iota(jnp.int32, (extra, q_ref.shape[1]), 0)
        open_ = (level <= qg_ref[0:1, :]) & (level >= qg_ref[1:2, :])
        qa_ref[HD:, :] = jnp.where(open_, 0.0, BLOCKED).astype(jnp.bfloat16)

    query = qa_ref[:, pl.ds(pl.multiple_of(step * width, 128), width)]

    def first(chunk, total):
        at = pl.ds(pl.multiple_of(chunk * size, 128), size)
        scores = lax.dot_general(
            ka_ref[:, at], query, (((0,), (0,)), ((), ())), preferred_element_type=jnp.float32
        )
        expd = jnp.exp(scores)
        exps[at, :] = expd
        return total + jnp.sum(expd, 0, keepdims=True)

    limit = limit_ref[step]
    total = lax.fori_loop(0, limit, first, jnp.zeros((1, width), jnp.float32))
    inverse = 1.0 / total
    inv_ref[...] = inverse

    def second(chunk, out):
        at = pl.ds(pl.multiple_of(chunk * size, 128), size)
        probs = (exps[at, :] * inverse).astype(jnp.bfloat16)
        return out + jnp.dot(v_ref[:, at], probs, preferred_element_type=jnp.float32)

    out = lax.fori_loop(0, limit, second, jnp.zeros((HD, width), jnp.float32))
    o_ref[...] = out.astype(jnp.bfloat16)


def query_width(keys):
    return 256 if keys <= 4096 else 128


def whole(shape):
    return pl.BlockSpec(shape, lambda step: (0,) * len(shape))


def kind_block(value, kind):
    return pl.BlockSpec((None,) + value.shape[1:], lambda step: (kind, 0, 0))


def attend_forward(own, everyone, query_groups, key_groups, extra, limits):
    queries, keys = own.shape[2], everyone.shape[2]
    width = query_width(keys)
    depth = HD + extra

    def part(rows):
        return pl.BlockSpec((rows, width), lambda step: (0, step))

    return pl.pallas_call(
        forward_kernel,
        grid=(queries // width,),
        out_shape=(
            jax.ShapeDtypeStruct((HD, queries), jnp.bfloat16),
            jax.ShapeDtypeStruct((1, queries), jnp.float32),
            jax.ShapeDtypeStruct((depth, queries), jnp.bfloat16),
            jax.ShapeDtypeStruct((depth, keys), jnp.bfloat16),
        ),
        in_specs=[
            pl.BlockSpec(memory_space=pltpu.SMEM),
            kind_block(own, 0),
            kind_block(everyone, 1),
            kind_block(everyone, 2),
            whole(query_groups.shape),
            whole(key_groups.shape),
        ],
        out_specs=(part(HD), part(1), whole((depth, queries)), whole((depth, keys))),
        scratch_shapes=[pltpu.VMEM((keys, width), jnp.float32)],
        compiler_params=pltpu.CompilerParams(
            vmem_limit_bytes=room(
                *(((depth, count), jnp.bfloat16) for count in (queries, keys) * 4),
                ((keys, width), jnp.float32),
                ((4 * HD, keys), jnp.float32),
            )
        ),
        name="attend_forward",
    )(limits, own, everyone, everyone, query_groups, key_groups)


def backward_kernel(
    limit_ref, qa_ref, ka_ref, v_ref, do_ref, inv_ref, dq_ref, dk_ref, dv_ref, probs_s, terms_s
):
    step = pl.program_id(0)
    width = dq_ref.shape[1]
    keys = v_ref.shape[1]
    size = chunks(keys)

    @pl.when(step == 0)
    def _():
        dk_ref[...] = jnp.zeros_like(dk_ref)
        dv_ref[...] = jnp.zeros_like(dv_ref)

    query = qa_ref[...]
    d_out = do_ref[...]
    inverse = inv_ref[...]

    def first(chunk, delta):
        at = pl.ds(pl.multiple_of(chunk * size, 128), size)
        scores = lax.dot_general(
            ka_ref[:, at], query, (((0,), (0,)), ((), ())), preferred_element_type=jnp.float32
        )
        probs = jnp.exp(scores) * inverse
        d_probs = lax.dot_general(
            v_ref[:, at], d_out, (((0,), (0,)), ((), ())), preferred_element_type=jnp.float32
        )
        terms = probs * d_probs
        probs_s[at, :] = probs
        terms_s[at, :] = terms
        return delta + jnp.sum(terms, 0, keepdims=True)

    limit = limit_ref[step]
    delta = lax.fori_loop(0, limit, first, jnp.zeros((1, width), jnp.float32))

    def second(chunk, d_query):
        at = pl.ds(pl.multiple_of(chunk * size, 128), size)
        probs = probs_s[at, :]
        d_scores = (terms_s[at, :] - probs * delta).astype(jnp.bfloat16)
        rows = (((1,), (1,)), ((), ()))
        dk_ref[:, at] += lax.dot_general(query[:HD], d_scores, rows, preferred_element_type=jnp.float32)
        dv_ref[:, at] += lax.dot_general(
            d_out, probs.astype(jnp.bfloat16), rows, preferred_element_type=jnp.float32
        )
        return d_query + jnp.dot(ka_ref[:HD, at], d_scores, preferred_element_type=jnp.float32)

    dq_ref[...] = lax.fori_loop(0, limit, second, jnp.zeros((HD, width), jnp.float32))


def attend_backward(qa, ka, everyone, d_out, inverse, limits):
    queries, keys = qa.shape[1], ka.shape[1]
    width = query_width(keys)

    def part(rows):
        return pl.BlockSpec((rows, width), lambda step: (0, step))

    return pl.pallas_call(
        backward_kernel,
        grid=(queries // width,),
        out_shape=(
            jax.ShapeDtypeStruct((HD, queries), jnp.float32),
            jax.ShapeDtypeStruct((HD, keys), jnp.float32),
            jax.ShapeDtypeStruct((HD, keys), jnp.float32),
        ),
        in_specs=[
            pl.BlockSpec(memory_space=pltpu.SMEM),
            part(qa.shape[0]),
            whole(ka.shape),
            kind_block(everyone, 2),
            part(HD),
            part(1),
        ],
        out_specs=(part(HD), whole((HD, keys)), whole((HD, keys))),
        scratch_shapes=[
            pltpu.VMEM((keys, width), jnp.float32),
            pltpu.VMEM((keys, width), jnp.float32),
        ],
        compiler_params=pltpu.CompilerParams(
            vmem_limit_bytes=room(
                *(((ka.shape[0], count), jnp.bfloat16) for count in (queries, keys) * 4),
                *(((keys, width), jnp.float32),) * 2,
                ((4 * HD, keys), jnp.float32),
            )
        ),
        name="attend_backward",
    )(limits, qa, ka, everyone, d_out, inverse)


def layer_mod(resid, shift, scale):
    centered = resid - jnp.mean(resid, -1, keepdims=True)
    normed = centered * lax.rsqrt(jnp.mean(centered * centered, -1, keepdims=True) + 1e-06)
    return normed * (1.0 + scale) + shift


def low(value):
    return lax.reduce_precision(value, 8, 7)


def norm_factor(value, axis):
    return lax.rsqrt(jnp.mean(value * value, axis, keepdims=True) + 1e-06)


def unit_back(grad, unit, factor):
    return factor * (grad - unit * jnp.mean(unit * grad, 0, keepdims=True))


def gelu_tanh(value):
    return jax.nn.gelu(value, approximate=True)


def contract(left, right, left_dim, right_dim):
    return lax.dot_general(
        left, right, (((left_dim,), (right_dim,)), ((), ())), preferred_element_type=jnp.float32
    )


def adamw(weight, first, second, grad, rate):
    first = 0.5 * first + 0.5 * grad
    second = 0.5 * second + 0.5 * grad * grad
    fix = 1.0 - 0.5**STEP
    update = first / fix / (jnp.sqrt(second / fix) + 1e-08)
    return (first, second, weight - rate * (update + 0.05 * weight))


def pick(value, index):
    return lax.dynamic_index_in_dim(value, index, 0, keepdims=False)


def per_device(
    codes,
    targets,
    tok_weights,
    group_ids,
    labels,
    tables_w,
    tables_m,
    tables_v,
    ada_w,
    ada_m,
    ada_v,
    attn_w,
    attn_m,
    attn_v,
    mlp_w,
    mlp_m,
    mlp_v,
    head_w,
    head_m,
    head_v,
    small_w,
    small_m,
    small_v,
):
    sizes = {axis: lax.axis_size(axis) for axis in AXES}
    seq = sizes["seq"]
    at_seq, at_tp, at_dp = (lax.axis_index(axis) for axis in AXES)
    bf16, f32 = jnp.bfloat16, jnp.float32
    tokens = codes.shape[1]
    block = tokens // 2
    width = ada_w.shape[1] // 8
    rows_own = tables_w.shape[1]
    owners = seq * 2
    rows, items = labels.shape
    quarter = head_w.shape[1] // 2
    head_cols = small_w.shape[1] // 2
    heads = head_cols // HD
    pairs = rows * heads

    def quarters(*weights):
        mine, other = [], []
        for value in weights:
            halves = value.astype(bf16).reshape(rows_own, 2, -1)
            mine.append(lax.dynamic_index_in_dim(halves, at_dp, 1, keepdims=False))
            other.append(lax.dynamic_index_in_dim(halves, 1 - at_dp, 1, keepdims=False))
        mine = jnp.concatenate(mine, 1)
        got = swapped(jnp.concatenate(other, 1), "dp")
        return jnp.where(
            at_dp == 0, jnp.concatenate([mine, got], 0), jnp.concatenate([got, mine], 0)
        )

    def everywhere(block):
        return lax.all_gather(block, "seq", axis=0, tiled=True)

    attn_block = quarters(attn_w[0], attn_w[1], attn_w[2], attn_w[3])
    codes, attn_block = lax.optimization_barrier((codes, attn_block))
    attn_all = everywhere(attn_block)
    w_qkv, w_out = jnp.split(attn_all, [3 * head_cols], 1)
    rest_block = quarters(mlp_w[0], mlp_w[1], head_w)
    codes, rest_block = lax.optimization_barrier((codes, rest_block))
    mlp_block, head_block = jnp.split(rest_block, [2 * quarter], 1)
    w_up, w_down = jnp.split(everywhere(mlp_block), 2, 1)
    w_head = everywhere(head_block)

    label_flat = labels.reshape(-1)
    class_ids = lax.broadcasted_iota(jnp.int32, (NCLS, 1), 0)
    classes = tables_w[V : V + NCLS].astype(bf16)
    cond_own = contract((class_ids == label_flat[None, :]).astype(bf16), classes, 0, 0)
    silu_own = low(jax.nn.silu(cond_own))
    ada = low(ada_w)
    mods_part = contract(silu_own.astype(bf16), ada.astype(bf16), 1, 0)
    mods_part = jnp.transpose(mods_part.reshape(rows * items, owners, -1), (1, 0, 2))

    groups_chunk = lax.dynamic_slice_in_dim(group_ids[0], at_seq * tokens, tokens)
    ints = jnp.stack([codes[0], targets[0], tok_weights[0], groups_chunk])
    levels = low(tables_w[V + NCLS :])
    slot = rows * items * (8 * width // owners)
    shared = [ints.astype(f32).reshape(-1), levels.reshape(-1)]
    extra = sum(value.size for value in shared)
    shared.append(jnp.zeros((-(slot + extra) % 1024,), f32))
    shared = jnp.broadcast_to(jnp.concatenate(shared)[None], (owners, (slot + extra + 1023) // 1024 * 1024 - slot))
    opening = jnp.concatenate([mods_part.reshape(owners, -1), shared], 1).reshape(owners, 8, -1)
    (opening,) = direct([(opening, True)], ("seq", "dp"), sizes, 1)
    opening = opening.reshape(owners, -1)
    mods_sum = opening[:, :slot].reshape(mods_part.shape)
    ints_all = opening[:, slot : slot + ints.size].astype(jnp.int32)
    levels = opening[:, slot + ints.size : slot + extra].reshape(owners, LEVELS, rows_own)
    levels = jnp.pad(levels.astype(bf16), ((0, 0), (0, 16 - LEVELS), (0, 0)))
    levels = jnp.transpose(levels, (1, 0, 2)).reshape(16, width)
    ints_all = ints_all.reshape(seq, rows, 4, tokens)
    own_ints = pick(ints_all, at_seq).reshape(rows, 4, 2, block)
    own_ints = jnp.where(at_dp == 0, own_ints, own_ints[::-1])
    own_ints = jnp.where(at_tp == 0, own_ints, own_ints[:, :, ::-1])
    own_ints = jnp.transpose(own_ints, (1, 0, 2, 3)).reshape(4, rows * tokens)
    weight_total = jnp.sum(ints_all[:, :, 2]).astype(f32)

    half_ints = ints_all.reshape(seq, rows, 4, 2, block)
    half_ints = lax.dynamic_index_in_dim(half_ints, at_tp, 3, keepdims=False)

    def one_hot(index, count):
        return (lax.broadcasted_iota(jnp.int32, (count, 1), 0) == index[None, :]).astype(bf16)

    looked = contract(tables_w[:V].astype(bf16), one_hot(half_ints[:, :, 0].reshape(-1), V), 0, 0).astype(bf16)
    looked = jnp.transpose(looked.reshape(rows_own, owners, block), (1, 0, 2))
    resid, mods_all = direct(
        [(looked, True), (jnp.sum(mods_sum, 0), False)], ("seq", "dp"), sizes, 2
    )
    level_of = own_ints[3, :block] % LEVELS
    resid = resid.reshape(width, block).T.astype(f32) + contract(one_hot(level_of, 16), levels, 0, 0)
    mods_all = jnp.transpose(mods_all, (1, 0, 2)).reshape(rows, items, 8, width)
    mods_own = pick(mods_all, at_dp)
    item_of = own_ints[3, :block] // LEVELS
    select = (item_of[:, None] == jnp.arange(items)[None, :]).astype(f32)

    def mod(part):
        return sum(select[:, i : i + 1] * mods_own[i, part][None, :] for i in range(items))

    mods_rows = mods_own.reshape(items * 8, width)
    select_lanes = jnp.pad(select, ((0, 0), (0, 128 - items)))

    def run_stage(mode, parts, terms, values, sums, number):
        return stage(
            mode, parts, items, sizes, terms, values, mods_rows, select_lanes, sums, number
        )

    both = ints_all.reshape(owners, 4, 2, block)
    both = jnp.where(at_tp == 0, both, both[:, :, ::-1])
    ids = [
        kind(both[:, index, side]).reshape(1, -1)
        for side in range(2)
        for index, kind in ((0, lambda value: value), (3, lambda value: value % LEVELS))
    ]
    h_one = group_gather(layer_mod(resid, mod(0), mod(1)).astype(bf16))
    qkv = contract(w_qkv, h_one, 0, 1).reshape(3, heads, HD, rows * tokens)
    bias = lax.dynamic_slice_in_dim(small_w, at_dp * head_cols, head_cols, 1)
    bias = bias.reshape(2, heads, HD, 1)
    q_raw, k_raw, v_raw = qkv[0] + bias[0], qkv[1], qkv[2] + bias[1]
    q_factor, k_factor = norm_factor(q_raw, 1), norm_factor(k_raw, 1)
    units = jnp.stack([q_raw * q_factor * 0.25, k_raw * k_factor, v_raw]).astype(bf16)
    factors = jnp.zeros((heads, 6, rows * tokens), f32)
    factors = jnp.concatenate([q_factor, k_factor, factors], 1)[None]
    pair_own, pair_factors = pair_exchange([units, factors], sizes, heads, tokens, True, 3)
    pair = at_seq % pairs
    row_groups = lax.dynamic_index_in_dim(ints_all[:, :, 3], pair // heads, 1, keepdims=False).reshape(1, -1)
    turns = seq // pairs
    same_pair = [[turn * pairs + index for turn in range(turns)] for index in range(pairs)]

    def own_keys(value):
        if turns == 1:
            return value
        return lax.psum_scatter(
            value, "seq", scatter_dimension=1, tiled=True, axis_index_groups=same_pair
        )

    pair_all = pair_own
    if turns > 1:
        pair_all = lax.all_gather(
            pair_own, "seq", axis=2, tiled=True, axis_index_groups=same_pair
        )
    query_groups = lax.dynamic_slice_in_dim(
        row_groups, at_seq // pairs * pairs * tokens, pairs * tokens, 1
    )
    query_groups = jnp.concatenate([query_groups, query_groups // LEVELS * LEVELS])
    extra = -(-items * LEVELS // 16) * 16
    key_levels = row_groups[0] % LEVELS
    top_levels = jnp.max((query_groups[0] % LEVELS).reshape(-1, query_width(seq * tokens)), 1)
    places = jnp.arange(1, seq * tokens + 1)
    reach = jnp.max(jnp.where(key_levels[None, :] <= top_levels[:, None], places[None, :], 0), 1)
    size = chunks(seq * tokens)
    limits = (reach + size - 1) // size
    out_pair, inverse, qa, ka = attend_forward(
        pair_own, pair_all, query_groups, row_groups, extra, limits
    )
    (heads_out,) = pair_exchange([out_pair[None]], sizes, heads, tokens, False, 4)
    heads_out = heads_out.reshape(head_cols, rows * tokens)
    attn_out, x_one, h_two = run_stage(
        "forward", (2, 3, 4), contract(heads_out, w_out, 0, 1), [resid], [], 10
    )
    up_val = contract(h_two, w_up, 1, 0)
    act = gelu_tanh(up_val).astype(bf16)
    mlp_out, x_two, h_three = run_stage(
        "forward", (5, 6, 7), contract(act, w_down, 1, 1), [x_one], [], 11
    )
    logits = contract(h_three, w_head, 1, 0)

    first_code = (at_tp * 2 + at_dp) * quarter
    hit = (own_ints[1][:, None] - first_code == jnp.arange(quarter)[None, :]).astype(f32)
    local_top = jnp.max(logits, 1)
    local_sum = jnp.sum(jnp.exp(logits - local_top[:, None]), 1)
    linear_part = 0.9 * jnp.sum(hit * logits, 1) + 0.1 / V * jnp.sum(logits, 1)
    stats = jnp.stack([local_top, local_sum, linear_part]).reshape(3, rows, 2, block)

    def stats_joined(one, two):
        top = jnp.maximum(one[0], two[0])
        total = one[1] * jnp.exp(one[0] - top) + two[1] * jnp.exp(two[0] - top)
        return jnp.stack([top, total, one[2] + two[2]])

    stats = stats_joined(stats, swapped(stats, "dp")[:, ::-1])
    stats = stats_joined(stats, swapped(stats, "tp")[:, :, ::-1])
    stats = stats.reshape(3, rows * tokens)
    log_total = stats[0] + jnp.log(stats[1])
    weights = own_ints[2].astype(f32)
    loss_part = jnp.sum((weights * (log_total - stats[2]))[:block])
    scale_rows = 128.0 * weights / weight_total
    probs = jnp.exp(logits - log_total[:, None])
    d_logits = (scale_rows[:, None] * (probs - 0.9 * hit - 0.1 / V)).astype(bf16)

    def scattered(value):
        return lax.psum_scatter(value, "seq", scatter_dimension=0, tiled=True).astype(f32)

    def by_place(value):
        return value.reshape(seq // 2, 2, 2 * rows_own, -1)

    d_h_three = contract(d_logits, w_head, 1, 1)
    cuts = [0, quarter * 4 // 8, quarter]
    head_parts = [
        by_place(contract(h_three, d_logits[:, first:last], 0, 0))
        for first, last in zip(cuts, cuts[1:])
    ]
    d_x_two, sums_three, d_mlp, grad_head_one = run_stage(
        "backward", (7, 5), d_h_three, [x_two, mlp_out], head_parts[:1], 12
    )
    d_act = contract(d_mlp, w_down, 1, 0)
    d_up = jax.vjp(gelu_tanh, up_val)[1](d_act)[0].astype(bf16)
    grad_mlp = outer([(h_two, d_up, 0), (d_mlp, act, 0)], bf16)
    grad_mlp, d_up = lax.optimization_barrier((grad_mlp, d_up))
    grad_mlp = scattered(grad_mlp)
    d_h_two = contract(d_up, w_up, 1, 1)
    d_x_one, sums_two, d_attn = run_stage(
        "backward", (4, 2), d_h_two, [x_one, attn_out, d_x_two], [], 13
    )
    d_heads = contract(w_out, d_attn, 0, 1).astype(bf16).reshape(1, heads, HD, rows * tokens)
    (d_out_pair,) = pair_exchange([d_heads], sizes, heads, tokens, True, 5)
    d_query, d_keys, d_values = attend_backward(qa, ka, pair_all, d_out_pair[0], inverse, limits)
    q_factor, k_factor = pair_factors[0, 0:1], pair_factors[0, 1:2]
    d_q = unit_back(d_query, pair_own[0].astype(f32) * 4.0, q_factor) * 0.25
    d_k = unit_back(own_keys(d_keys), pair_own[1].astype(f32), k_factor)
    stacked = jnp.stack([d_q, d_k, own_keys(d_values)]).astype(bf16)
    (d_qkv,) = pair_exchange([stacked], sizes, heads, tokens, False, 6)
    d_qkv = d_qkv.reshape(3 * head_cols, rows * tokens)
    grad_attn = outer([(h_one, d_qkv, 1), (d_attn, heads_out, 1)], f32)
    bias_sums = jnp.sum(d_qkv.astype(f32), 1).reshape(3, head_cols)[::2]
    d_resid, sums_one, grad_head_two = run_stage(
        "last",
        (1,),
        contract(d_qkv, w_qkv, 0, 1),
        [resid, d_x_one],
        head_parts[1:],
        14,
    )

    gate = 2 * items
    d_mods = jnp.concatenate(
        [sums_one, sums_two[gate:], sums_two[:gate], sums_three[gate:], sums_three[:gate]], 0
    )
    d_mods = d_mods.reshape(8, items, owners // 8, -1)
    d_mods = jnp.transpose(d_mods, (0, 2, 1, 3)).reshape(owners, items, -1)
    d_cols = d_resid.T.reshape(owners, rows_own, block)
    slot = d_mods.shape[2]
    bias_row = jnp.pad(bias_sums.reshape(-1), (0, -bias_sums.size % slot)).reshape(-1, slot)
    d_mods = jnp.concatenate([d_mods, jnp.broadcast_to(bias_row, (owners,) + bias_row.shape)], 1)
    d_mods, d_mods_in, grad_attn, g_codes, g_levels = tail_stage(
        d_cols, d_mods, items, by_place(grad_attn), ids, sizes, 8
    )
    bias_sums = d_mods_in[:, items:].reshape(owners, -1)[:, : 2 * head_cols]
    bias_sums = jnp.sum(bias_sums.reshape(seq, 2, 2, head_cols), 0)
    g_small = jnp.concatenate([bias_sums[0], bias_sums[1]], 1)
    d_mods = d_mods.reshape(owners, rows * items, -1)
    d_mods = jnp.transpose(d_mods, (1, 0, 2)).reshape(rows * items, 8 * width)
    g_ada = sum(silu_own[i][:, None] * d_mods[i][None, :] for i in range(rows * items))
    d_silu = jnp.stack([jnp.sum(ada * d_mods[i][None, :], 1) for i in range(rows * items)])
    d_cond = jax.vjp(jax.nn.silu, cond_own)[1](d_silu)[0]

    class_lanes = lax.broadcasted_iota(jnp.int32, (1, NCLS), 1)
    g_classes = sum(
        jnp.where(class_lanes == label_flat[i], d_cond[i][:, None], 0.0) for i in range(rows * items)
    )
    g_tables = jnp.concatenate([g_codes, g_classes, g_levels[:, :LEVELS]], 1).T

    def owned(value):
        parts = value.reshape(2, rows_own, -1)
        mine = pick(parts, at_dp)
        return mine, swapped(pick(parts, 1 - at_dp), "dp")

    def joined(pair, first, count):
        mine, got = (part[:, first : first + count] for part in pair)
        return jnp.where(
            at_dp == 0, jnp.concatenate([mine, got], 1), jnp.concatenate([got, mine], 1)
        )

    def side_by_side(value, first, count):
        other = value.shape[1] // 2 + first
        return [value[:, first : first + count], value[:, other : other + count]]

    g_attn = jnp.stack(
        [
            jnp.concatenate(side_by_side(grad_attn, kind * head_cols, head_cols), 1)
            for kind in range(4)
        ]
    )
    mlp_pair = owned(grad_mlp)
    g_mlp = jnp.stack([joined(mlp_pair, kind * quarter, quarter) for kind in range(2)])
    one, two = (
        side_by_side(value, 0, value.shape[1] // 2) for value in (grad_head_one, grad_head_two)
    )
    g_head = jnp.concatenate([one[0], two[0], one[1], two[1]], 1)

    local_squares = (jnp.sum(g_tables * g_tables) + jnp.sum(g_ada * g_ada)) / 2
    local_squares = (
        local_squares
        + sum(
            jnp.sum(value * value)
            for value in (grad_attn, grad_mlp, grad_head_one, grad_head_two)
        )
    )
    local_squares = local_squares + jnp.sum(g_small * g_small) / owners
    column = lax.broadcasted_iota(jnp.int32, (8, 128), 1)
    scalars = jnp.where(column == 0, local_squares, jnp.where(column == 1, loss_part, 0.0))
    scalars = jnp.sum(direct([(scalars, False)], AXES, sizes, 9)[0], 0)
    grad_norm = jnp.sqrt(scalars[0, 0])
    loss = 128.0 * scalars[0, 1] / weight_total
    factor = jnp.minimum(1.0, 1.0 / (grad_norm + 1e-06))
    tables_n = adamw(tables_w, tables_m, tables_v, g_tables * factor, 0.3)
    ada_n = adamw(ada_w, ada_m, ada_v, g_ada * factor, 0.03)
    attn_n = adamw(attn_w, attn_m, attn_v, g_attn * factor, 0.1)
    mlp_n = adamw(mlp_w, mlp_m, mlp_v, g_mlp * factor, 0.02)
    head_n = adamw(head_w, head_m, head_v, g_head * factor, 0.03)
    small_n = adamw(small_w, small_m, small_v, g_small * factor, 0.5)
    return (
        loss,
        grad_norm,
        *tables_n,
        *ada_n,
        *attn_n,
        attn_n[2].astype(bf16),
        *mlp_n,
        mlp_n[2].astype(bf16),
        *head_n,
        head_n[2].astype(bf16),
        *small_n,
    )


def solution(mesh):
    tokens, whole_rows = P("dp", "seq"), P("dp", None)
    tables, ada = P(None, ("seq", "dp")), P(("seq", "dp"), None)
    layer, head, small = P(None, ("seq", "dp"), "tp"), P(("seq", "dp"), "tp"), P(None, "tp")
    return jax.shard_map(
        per_device,
        mesh=mesh,
        in_specs=(
            (tokens,) * 3
            + (whole_rows, P())
            + (tables,) * 3
            + (ada,) * 3
            + (layer,) * 6
            + (head,) * 3
            + (small,) * 3
        ),
        out_specs=(
            (P(), P())
            + (tables,) * 3
            + (ada,) * 3
            + (layer,) * 8
            + (head,) * 4
            + (small,) * 3
        ),
        check_vma=False,
    )
```
